256 devices in a mesh: seq: 128 (over y_lo, x, z, core), ch: 2 (over y_hi).
Axes of the slice: x: 4, y: 4 (y_hi: 2, y_lo: 2; y = y_hi * 2 + y_lo), z: 8, core: 2. Of those that a mesh axis runs over, the one named last changes fastest.
Arguments:
- signal: bfloat16 [262144, 768], P('seq', 'ch'), may hold values from -6 to 6
- gate: bfloat16 [262144, 768], P('seq', 'ch'), may hold values from -6 to 6
- kernel: bfloat16 [64, 2, 2048, 768], P(None, None, 'seq', 'ch'), may hold values from -6 to 6
- fwd_inner: bfloat16 [64, 64], replicated, may hold values from -0.75 to 0.75
- fwd_middle: bfloat16 [64, 64], replicated, may hold values from -0.75 to 0.75
- fwd_outer: bfloat16 [64, 64], replicated, may hold values from -0.75 to 0.75
- inv_outer: bfloat16 [64, 64], replicated, may hold values from -0.75 to 0.75
- inv_middle: bfloat16 [64, 64], replicated, may hold values from -0.75 to 0.75
- inv_inner: bfloat16 [64, 64], replicated, may hold values from -0.75 to 0.75
- tw_inner: float32 [64, 64], replicated, may hold values from 0.5 to 1.5
- tw_middle: float32 [64, 64], replicated, may hold values from 0.5 to 1.5
- itw_middle: float32 [64, 64], replicated, may hold values from 0.5 to 1.5
- itw_inner: float32 [64, 64], replicated, may hold values from 0.5 to 1.5
- skip: float32 [768], P('ch'), may hold values from -1 to 1
- w_out: bfloat16 [768, 1536], P('ch'), may hold values from -0.21875 to 0.21875
Outputs:
- mixed: bfloat16 [262144, 1536], P('seq', 'ch')
The draws below stay inside these ranges and needn't reach their ends.
All inputs are finite; a program needn't handle non-finite values.
Results may differ from the reference program's by a relative error of at most 0.0077.
Values may be sent and summed in bfloat16 or wider, within the bound.
A program may use at most 128 MiB of HBM per device.

```python
import math
import jax
import jax.numpy as jnp
from jax import lax

BLK = 64
DW = 768
DM = 1536
TOK_DEV = 2048
Q = 64
L = 262144


def block_scale(key, dims, split, least, high):
    loudness = 1.0
    for dim, shards_of in split:
        heights = jax.random.uniform(jax.random.fold_in(jax.random.fold_in(key, 6), dim), (shards_of,), jnp.float32, least / len(split), high / len(split))
        loudness = loudness * jnp.repeat(jnp.exp(heights), dims[dim] // shards_of).reshape((-1,) + (1,) * (len(dims) - 1 - dim))
    return loudness


def noise(rng, extent, scale, bound, pieces=(), dtype=jnp.bfloat16):
    result = jax.random.normal(rng, extent, jnp.float32) * scale
    if len(pieces) > 0:
        result = block_scale(rng, extent, pieces, -0.22, 0.18) * result
    return jnp.clip(result, min=-bound, max=bound).astype(dtype)


def setup_inputs(seed: int = 0) -> dict:
    key_list = jax.random.split(jax.random.key(seed), 16)
    return {
        "signal": noise(key_list[0], (L, DW), 1.0, 6.0, ((0, 128), (1, 2))),
        "gate": noise(key_list[1], (L, DW), 1.0, 6.0, ((0, 128), (1, 2))),
        "kernel": noise(key_list[2], (Q, 2, TOK_DEV, DW), 1.0, 6.0, ((2, 128), (3, 2))),
        "fwd_inner": noise(key_list[3], (BLK, BLK), BLK ** -0.5, 0.75),
        "fwd_middle": noise(key_list[4], (BLK, BLK), BLK ** -0.5, 0.75),
        "fwd_outer": noise(key_list[5], (Q, Q), Q ** -0.5, 0.75),
        "inv_outer": noise(key_list[6], (Q, Q), Q ** -0.5, 0.75),
        "inv_middle": noise(key_list[7], (BLK, BLK), BLK ** -0.5, 0.75),
        "inv_inner": noise(key_list[8], (BLK, BLK), BLK ** -0.5, 0.75),
        "tw_inner": jnp.clip(jax.random.uniform(key_list[9], (BLK, BLK), jnp.float32, 0.5, 1.5), 0.5, 1.5),
        "tw_middle": jnp.clip(jax.random.uniform(key_list[10], (Q, BLK), jnp.float32, 0.5, 1.5), 0.5, 1.5),
        "itw_middle": jnp.clip(jax.random.uniform(key_list[11], (Q, BLK), jnp.float32, 0.5, 1.5), 0.5, 1.5),
        "itw_inner": jnp.clip(jax.random.uniform(key_list[12], (BLK, BLK), jnp.float32, 0.5, 1.5), 0.5, 1.5),
        "skip": jnp.clip(jax.random.uniform(key_list[13], (DW,), jnp.float32, -1.0, 1.0) * block_scale(key_list[13], (DW,), ((0, 2),), -0.4, 0.0), -1.0, 1.0),
        "w_out": noise(key_list[14], (DW, DM), DW ** -0.5, 0.21875, ((0, 2),)),
    }


def reference(signal, gate, kernel, fwd_inner, fwd_middle, fwd_outer, inv_outer, inv_middle, inv_inner, tw_inner, tw_middle, itw_middle, itw_inner, skip, w_out):
    f32 = jnp.float32
    bf16 = jnp.bfloat16
    block = math.gcd(DW, 64)
    nblock = DW // block
    half = BLK // 2
    sig_blocks = signal.reshape(L, nblock, block).transpose(1, 0, 2)
    gate_blocks = gate.reshape(L, nblock, block).transpose(1, 0, 2)
    ker_blocks = kernel.reshape(Q, 2, TOK_DEV, nblock, block).transpose(3, 0, 1, 2, 4)
    skip_blocks = skip.reshape(nblock, block)
    fi = fwd_inner.astype(f32)
    fm = fwd_middle.astype(f32)
    fo = fwd_outer.astype(f32)
    io = inv_outer.astype(f32)
    im = inv_middle.astype(f32)
    ii = inv_inner.astype(f32)

    def mix_block(operands):
        sig, gat, ker, skp = operands
        u = sig.astype(f32).reshape(Q, BLK, BLK, block)
        first = (jnp.einsum('kc,abcn->abkn', fi, u) * tw_inner[None, :, :, None]).astype(bf16)
        second = (jnp.einsum('jb,abkn->ajkn', fm, first.astype(f32)) * tw_middle[:, :, None, None]).astype(bf16)
        kfull = ker.reshape(Q, 2, BLK, half, block).transpose(0, 2, 3, 1, 4).reshape(Q, BLK, BLK, block)
        spectrum = (jnp.einsum('ia,ajkn->ijkn', fo, second.astype(f32)) * kfull.astype(f32)).astype(bf16)
        back_outer = (jnp.einsum('ai,ijkn->ajkn', io, spectrum.astype(f32)) * itw_middle[:, :, None, None]).astype(bf16)
        back_middle = (jnp.einsum('bj,ajkn->abkn', im, back_outer.astype(f32)) * itw_inner[None, :, :, None]).astype(bf16)
        conv = jnp.einsum('ck,abkn->abcn', ii, back_middle.astype(f32)).reshape(L, block)
        act = jax.nn.silu(gat.astype(f32)) * (conv + skp[None, :] * sig.astype(f32))
        return act.astype(bf16)

    acts = lax.map(mix_block, (sig_blocks, gate_blocks, ker_blocks, skip_blocks))
    act = acts.transpose(1, 0, 2).reshape(L, DW)
    rows = BLK * BLK
    act_rows = act.reshape(L // rows, rows, DW)

    def project(piece):
        return jnp.dot(piece, w_out, preferred_element_type=f32).astype(bf16)

    return lax.map(project, act_rows).reshape(L, DM)
```

```python
import functools

import jax
import jax.numpy as jnp
from jax import lax
from jax.experimental import pallas as pl
from jax.experimental.pallas import tpu as pltpu
from jax.sharding import PartitionSpec as P

MESH = pl.DeviceIdType.MESH
F32 = jnp.float32
BF16 = jnp.bfloat16
LANES = 128
SUB = 16
NZ = 8
NXY = 8
NX = 4


def iota(shape, dim):
    return lax.broadcasted_iota(jnp.int32, shape, dim)


def one_hot(cond):
    return jnp.where(cond, 1.0, 0.0).astype(BF16)


def dot(a, b):
    return jnp.dot(a, b, preferred_element_type=F32)


def kernel(
    signal,
    gate,
    spectral,
    fwd_inner,
    fwd_middle,
    fwd_outer,
    inv_outer,
    inv_middle,
    inv_inner,
    tw_inner,
    tw_middle,
    itw_middle,
    itw_inner,
    skip,
    w_out,
    act_out,
    w_cat,
    sig,
    gat,
    ker,
    silu,
    rows_a,
    send_a,
    send_z,
    recv_z,
    recv_xy,
    spec,
    send_xy2,
    recv_xy2,
    recv_z2,
    send_j,
    rows_j,
    act,
    mat_in,
    mat_inv,
    mat_m,
    mat_f,
    mat_i,
    mat_im,
    t_in,
    t_mid,
    t_imid,
    t_iin,
    load_sem,
    local_sem,
    core_send,
    core_recv,
    z_send,
    z_recv,
    xy_send,
    xy_recv,
    xy2_send,
    xy2_recv,
    z2_send,
    z2_recv,
    core2_send,
    core2_recv,
    act_send,
    act_recv,
    w_send,
    w_recv,
    out_sem,
):
    nch = sig.shape[0]
    me = lax.axis_index("seq")
    ch = lax.axis_index("ch")
    core = me % 2
    chip = me // 2
    z = chip % NZ
    yx = chip // NZ
    y, x = yx // NX, yx % NX

    def at_z(d):
        other = (z + d) % NZ
        return other, ((yx * NZ + other) * 2 + core, ch)

    def at_xy(e):
        other = (y + e // NX) % 2 * NX + (x + e % NX) % NX
        return other, ((other * NZ + z) * 2 + core, ch)

    twin = (chip * 2 + 1 - core, ch)
    mate = (me, 1 - ch)

    def remote(src, dst, send, recv, device):
        return pltpu.make_async_remote_copy(
            src_ref=src,
            dst_ref=dst,
            send_sem=send,
            recv_sem=recv,
            device_id=device,
            device_id_type=MESH,
        )

    loads = []
    for i in range(nch):
        cols = pl.ds(i * LANES, LANES)
        trio = (
            pltpu.make_async_copy(signal.at[:, cols], sig.at[i], load_sem.at[0, i]),
            pltpu.make_async_copy(spectral.at[:, :, :, cols], ker.at[i], load_sem.at[1, i]),
            pltpu.make_async_copy(gate.at[:, cols], gat.at[i], load_sem.at[2, i]),
        )
        loads.append(trio)
    for kind in range(3):
        for i in range(nch):
            loads[i][kind].start()

    barrier = pltpu.get_barrier_semaphore()
    pl.semaphore_signal(barrier, inc=1, device_id=twin, device_id_type=MESH)
    pl.semaphore_signal(barrier, inc=1, device_id=mate, device_id_type=MESH)
    for d in range(1, NZ):
        pl.semaphore_signal(barrier, inc=1, device_id=at_z(d)[1], device_id_type=MESH)
    for e in range(1, NXY):
        pl.semaphore_signal(barrier, inc=1, device_id=at_xy(e)[1], device_id_type=MESH)

    def digit_k(q, flip):
        half = (q >> 5) ^ flip
        return 2 * (half * SUB + (q & 15)) + ((q >> 4) & 1)

    def expand(source, out, row_digit, col_digit, keep, block):
        size = out.shape[0]
        place = one_hot(iota((64, size), 0) == col_digit(iota((64, size), 1)))

        def body(n, carry):
            base = n * block
            pick = one_hot(iota((block, 64), 1) == row_digit(iota((block, 64), 0) + base))
            wide = dot(dot(pick, source[...]).astype(BF16), place)
            r = iota((block, size), 0) + base
            out[pl.ds(pl.multiple_of(base, block), block), :] = jnp.where(
                keep(r, iota((block, size), 1)), wide, 0.0
            ).astype(BF16)
            return carry

        lax.fori_loop(0, size // block, body, 0)

    def same_block(r, s):
        return (r >> 6) == (s >> 6)

    def same_sub(r, s):
        return (r & 15) == (s & 15)

    def in_z_order(q):
        return (q & 7) * 8 + (q >> 3)

    expand(fwd_inner, mat_in, lambda r: digit_k(r & 63, core), lambda s: s & 63, same_block, 128)

    def tw_in_body(n, carry):
        row = tw_inner[pl.ds(core * 32 + n, 1), :]
        hit = iota((64, 64), 1) == digit_k(iota((64, 64), 0), core)
        col = jnp.sum(jnp.where(hit, row, 0.0), axis=1, keepdims=True)
        t_in[pl.ds(pl.multiple_of(n * 64, 64), 64), :] = jnp.broadcast_to(col, (64, LANES))
        return carry

    lax.fori_loop(0, 32, tw_in_body, 0)

    def stage_inner(i):
        loads[i][0].wait()

        def body(n, carry):
            base = pl.multiple_of(n * 512, 512)
            wide = jnp.concatenate(
                [sig[i, pl.ds(base, 256), :], sig[i, pl.ds(base + 256, 256), :]], axis=1
            )
            res = dot(mat_in[...], wide)
            for s in range(2):
                part = res[:, s * LANES : (s + 1) * LANES] * t_in[pl.ds(base + 256 * s, 256), :]
                part = part.astype(BF16).reshape(4, 2, 2, SUB, LANES)
                b = n * 8 + s * 4
                rows_a[i, pl.ds(core * 32 + b, 4)] = part[:, 0]
                send_a[i, pl.ds(b, 4)] = part[:, 1]
            return carry

        lax.fori_loop(0, 4, body, 0)

    def core_copy(i):
        return remote(
            send_a.at[i],
            rows_a.at[i, pl.ds(core * 32, 32)],
            core_send.at[i],
            core_recv.at[i],
            twin,
        )

    stage_inner(0)
    pl.semaphore_wait(barrier, 2 + NZ - 1 + NXY - 1)
    core_copies = [core_copy(i) for i in range(nch)]
    core_copies[0].start()
    expand(fwd_middle, mat_m, lambda r: in_z_order(r >> 4), lambda s: s >> 4, same_sub, 128)
    tm_row = tw_middle[pl.ds(chip, 1), :]
    for n in range(4):
        hit = iota((256, 64), 1) == in_z_order((iota((256, 64), 0) + n * 256) >> 4)
        col = jnp.sum(jnp.where(hit, tm_row, 0.0), axis=1, keepdims=True)
        t_mid[n * 256 : (n + 1) * 256, :] = jnp.broadcast_to(col, (256, LANES))

    def pair(ref, i):
        v = ref[i].reshape(64, 2, SUB, LANES)
        return jnp.concatenate(
            [v[:, 0].reshape(64 * SUB, LANES), v[:, 1].reshape(64 * SUB, LANES)], axis=1
        )

    def apply(matrix, wide, finish):
        def body(n, carry):
            base = pl.multiple_of(n * 256, 256)
            finish(n, base, dot(matrix[pl.ds(base, 256), :], wide))
            return carry

        lax.fori_loop(0, 4, body, 0)

    def stage_middle(i):
        core_copies[i].wait_recv()

        def finish(n, base, res):
            for p in range(2):
                part = res[:, p * LANES : (p + 1) * LANES] * t_mid[pl.ds(base, 256), :]
                send_z[i, pl.ds(n * 2, 2), :, p] = part.astype(BF16).reshape(2, NXY, SUB, LANES)

        apply(mat_m, pair(rows_a, i), finish)

    order_z = (4, 3, 5, 2, 6, 1, 7)
    order_xy = (6, 2, 5, 7, 1, 3, 4)
    z_copies, xy_copies, xy2_copies, z2_copies = {}, {}, {}, {}

    def start_z(i):
        z_copies[i] = []
        for d in order_z:
            other, device = at_z(d)
            copy = remote(
                send_z.at[i, other], recv_z.at[i, z], z_send.at[i, d], z_recv.at[i, d], device
            )
            copy.start()
            z_copies[i].append(copy)
        own = pltpu.make_async_copy(send_z.at[i, z], recv_z.at[i, z], local_sem.at[0, i])
        own.start()
        z_copies[i].append(own)

    def start_xy(i):
        for copy in z_copies[i][:-1]:
            copy.wait_recv()
        z_copies[i][-1].wait()
        xy_copies[i] = []
        for e in order_xy:
            other, device = at_xy(e)
            copy = remote(
                recv_z.at[i, :, other],
                recv_xy.at[i, yx],
                xy_send.at[i, e],
                xy_recv.at[i, e],
                device,
            )
            copy.start()
            xy_copies[i].append(copy)
        own = pltpu.make_async_copy(recv_z.at[i, :, yx], recv_xy.at[i, yx], local_sem.at[1, i])
        own.start()
        xy_copies[i].append(own)

    def stage_outer(i):
        for copy in xy_copies[i][:-1]:
            copy.wait_recv()
        xy_copies[i][-1].wait()
        loads[i][1].wait()

        def product(n, base, res):
            factor = ker[i, pl.ds(n * 16, 16)]
            for p in range(2):
                part = res[:, p * LANES : (p + 1) * LANES].reshape(16, SUB, LANES)
                part = part * factor[:, p].astype(F32)
                spec[pl.ds(base, 256), p * LANES : (p + 1) * LANES] = part.astype(BF16).reshape(
                    256, LANES
                )

        apply(mat_f, pair(recv_xy, i), product)

        def finish(n, base, res):
            for p in range(2):
                part = res[:, p * LANES : (p + 1) * LANES] * t_imid[pl.ds(base, 256), :]
                send_xy2[i, pl.ds(n * 2, 2), :, p] = part.astype(BF16).reshape(2, NZ, SUB, LANES)

        apply(mat_i, spec[...], finish)

    def start_xy2(i):
        xy2_copies[i] = []
        for e in order_xy:
            other, device = at_xy(e)
            copy = remote(
                send_xy2.at[i, other],
                recv_xy2.at[i, yx],
                xy2_send.at[i, e],
                xy2_recv.at[i, e],
                device,
            )
            copy.start()
            xy2_copies[i].append(copy)
        own = pltpu.make_async_copy(send_xy2.at[i, yx], recv_xy2.at[i, yx], local_sem.at[2, i])
        own.start()
        xy2_copies[i].append(own)

    def start_z2(i):
        for copy in xy2_copies[i][:-1]:
            copy.wait_recv()
        xy2_copies[i][-1].wait()
        z2_copies[i] = []
        for d in order_z:
            other, device = at_z(d)
            copy = remote(
                recv_xy2.at[i, :, other],
                recv_z2.at[i, z],
                z2_send.at[i, d],
                z2_recv.at[i, d],
                device,
            )
            copy.start()
            z2_copies[i].append(copy)
        own = pltpu.make_async_copy(recv_xy2.at[i, :, z], recv_z2.at[i, z], local_sem.at[3, i])
        own.start()
        z2_copies[i].append(own)

    def core2_copy(i):
        return remote(
            send_j.at[i], rows_j.at[i, :, core], core2_send.at[i], core2_recv.at[i], twin
        )

    core2_copies = [core2_copy(i) for i in range(nch)]

    def stage_inv_middle(i):
        for copy in z2_copies[i][:-1]:
            copy.wait_recv()
        z2_copies[i][-1].wait()

        wide = pair(recv_z2, i)

        def block(n, target):
            base = pl.multiple_of(n * 256, 256)
            res = dot(mat_im[pl.ds(base, 256), :], wide)
            for p in range(2):
                part = res[:, p * LANES : (p + 1) * LANES] * t_iin[p, pl.ds(base, 256), :]
                target(n, p, part.astype(BF16).reshape(16, SUB, LANES))

        def to_twin(n, p, part):
            send_j[i, pl.ds((n - 2) * 16, 16), p] = part

        def to_own(n, p, part):
            rows_j[i, pl.ds(n * 16, 16), core, p] = part

        lax.fori_loop(2, 4, lambda n, c: (block(n, to_twin), c)[1], 0)
        core2_copies[i].start()
        lax.fori_loop(0, 2, lambda n, c: (block(n, to_own), c)[1], 0)

    act_copies = [
        remote(act.at[i], act_out.at[:, pl.ds((nch + i) * LANES, LANES)], act_send.at[i], act_recv.at[i], mate)
        for i in range(nch)
    ]
    own_outs = [
        pltpu.make_async_copy(act.at[i], act_out.at[:, pl.ds(i * LANES, LANES)], out_sem.at[i])
        for i in range(nch)
    ]

    def stage_inv_inner(i):
        core2_copies[i].wait_recv()
        scale = skip[0:1, i * LANES : (i + 1) * LANES]

        def body(n, carry):
            base = pl.multiple_of(n * 512, 512)
            left = rows_j[i, pl.ds(n * 8, 4)].reshape(256, LANES)
            right = rows_j[i, pl.ds(n * 8 + 4, 4)].reshape(256, LANES)
            res = dot(mat_inv[...], jnp.concatenate([left, right], axis=1))
            for s in range(2):
                at = pl.ds(base + 256 * s, 256)
                conv = res[:, s * LANES : (s + 1) * LANES]
                conv = conv + scale * sig[i, at, :].astype(F32)
                act[i, at, :] = (silu[i, at, :] * conv).astype(BF16)
            return carry

        lax.fori_loop(0, 4, body, 0)
        act_copies[i].start()
        own_outs[i].start()

    def make_silu(i):
        loads[i][2].wait()

        def body(n, carry):
            at = pl.ds(pl.multiple_of(n * 256, 256), 256)
            g = gat[i, at, :].astype(F32)
            silu[i, at, :] = g / (1.0 + jnp.exp(-g))
            return carry

        lax.fori_loop(0, 8, body, 0)

    def tw_imid_body(n, carry):
        row = itw_middle[pl.ds(n, 1), :]
        col = jnp.sum(jnp.where(iota((SUB, 64), 1) == chip, row, 0.0), axis=1, keepdims=True)
        t_imid[pl.ds(pl.multiple_of(n * SUB, SUB), SUB), :] = jnp.broadcast_to(col, (SUB, LANES))
        return carry

    def tw_iin_body(n, carry):
        row = itw_inner[pl.ds(((n >> 5) ^ core) * 32 + (n & 31), 1), :]
        for p in range(2):
            hit = iota((SUB, 64), 1) == 2 * (core * SUB + iota((SUB, 64), 0)) + p
            col = jnp.sum(jnp.where(hit, row, 0.0), axis=1, keepdims=True)
            t_iin[p, pl.ds(pl.multiple_of(n * SUB, SUB), SUB), :] = jnp.broadcast_to(
                col, (SUB, LANES)
            )
        return carry

    stage_middle(0)
    start_z(0)
    for i in range(1, nch):
        stage_inner(i)
        core_copies[i].start()
    width = w_cat.shape[1]
    w_copy = remote(
        w_out.at[:, pl.ds(pl.multiple_of((1 - ch) * width, width), width)],
        w_cat.at[pl.ds(w_out.shape[0], w_out.shape[0])],
        w_send,
        w_recv,
        mate,
    )
    w_copy.start()
    w_own = pltpu.make_async_copy(
        w_out.at[:, pl.ds(pl.multiple_of(ch * width, width), width)],
        w_cat.at[pl.ds(0, w_out.shape[0])],
        out_sem.at[nch],
    )
    w_own.start()
    stage_middle(1)
    start_z(1)
    stage_middle(2)
    expand(fwd_outer, mat_f, lambda r: r >> 4, lambda s: s >> 4, same_sub, 128)
    expand(inv_outer, mat_i, lambda r: r >> 4, lambda s: s >> 4, same_sub, 128)
    lax.fori_loop(0, 64, tw_imid_body, 0)
    start_xy(0)
    start_z(2)
    expand(
        inv_middle,
        mat_im,
        lambda r: (r >> 4) ^ (core * 32),
        lambda s: in_z_order(s >> 4),
        same_sub,
        128,
    )
    expand(inv_inner, mat_inv, lambda r: r & 63, lambda s: digit_k(s & 63, 0), same_block, 128)
    lax.fori_loop(0, 64, tw_iin_body, 0)
    stage_outer(0)
    start_xy2(0)
    for i in range(nch):
        make_silu(i)
    start_xy(1)
    start_z2(0)
    stage_outer(1)
    start_xy2(1)
    start_xy(2)
    start_z2(1)
    stage_outer(2)
    start_xy2(2)
    stage_inv_middle(0)
    stage_inv_inner(0)
    start_z2(2)
    stage_inv_middle(1)
    stage_inv_inner(1)
    stage_inv_middle(2)
    stage_inv_inner(2)

    for i in range(nch):
        core_copies[i].wait_send()
        core2_copies[i].wait_send()
        for table in (z_copies, xy_copies, xy2_copies, z2_copies):
            for copy in table[i][:-1]:
                copy.wait_send()
        own_outs[i].wait()
        act_copies[i].wait()
    w_own.wait()
    w_copy.wait()


def on_device(*args):
    signal, kernel_arr, skip, w_out = args[0], args[2], args[13], args[14]
    tokens, nchan = signal.shape
    nch = nchan // LANES
    width = w_out.shape[1] // 2
    small = pl.BlockSpec(memory_space=pltpu.VMEM)
    big = pl.BlockSpec(memory_space=pl.ANY)
    specs = [big, big, big] + [small] * 11 + [big]
    chunk = (nch, 64, 2, SUB, LANES)
    square = pltpu.VMEM((64 * SUB, 64 * SUB), BF16)
    dma = pltpu.SemaphoreType.DMA
    scratch = [
        pltpu.VMEM((nch, tokens, LANES), BF16),
        pltpu.VMEM((nch, tokens, LANES), BF16),
        pltpu.VMEM(chunk, BF16),
        pltpu.VMEM((nch, tokens, LANES), F32),
        pltpu.VMEM(chunk, BF16),
        pltpu.VMEM((nch, 32, 2, SUB, LANES), BF16),
        pltpu.VMEM((nch, NZ, NXY, 2, SUB, LANES), BF16),
        pltpu.VMEM((nch, NZ, NXY, 2, SUB, LANES), BF16),
        pltpu.VMEM((nch, NXY, NZ, 2, SUB, LANES), BF16),
        pltpu.VMEM((64 * SUB, 2 * LANES), BF16),
        pltpu.VMEM((nch, NXY, NZ, 2, SUB, LANES), BF16),
        pltpu.VMEM((nch, NXY, NZ, 2, SUB, LANES), BF16),
        pltpu.VMEM((nch, NZ, NXY, 2, SUB, LANES), BF16),
        pltpu.VMEM((nch, 32, 2, SUB, LANES), BF16),
        pltpu.VMEM((nch, 32, 2, 2, SUB, LANES), BF16),
        pltpu.VMEM((nch, tokens, LANES), BF16),
        pltpu.VMEM((256, 256), BF16),
        pltpu.VMEM((256, 256), BF16),
        square,
        square,
        square,
        square,
        pltpu.VMEM((tokens, LANES), F32),
        pltpu.VMEM((64 * SUB, LANES), F32),
        pltpu.VMEM((64 * SUB, LANES), F32),
        pltpu.VMEM((2, 64 * SUB, LANES), F32),
        dma((3, nch)),
        dma((4, nch)),
        dma((nch,)),
        dma((nch,)),
        dma((nch, NZ)),
        dma((nch, NZ)),
        dma((nch, NXY)),
        dma((nch, NXY)),
        dma((nch, NXY)),
        dma((nch, NXY)),
        dma((nch, NZ)),
        dma((nch, NZ)),
        dma((nch,)),
        dma((nch,)),
        dma((nch,)),
        dma((nch,)),
        dma(()),
        dma(()),
        dma((nch + 1,)),
    ]
    operands = list(args)
    operands[13] = skip.reshape(1, nchan)
    act, w_cat = pl.pallas_call(
        kernel,
        out_shape=(
            jax.ShapeDtypeStruct((tokens, 2 * nchan), BF16),
            jax.ShapeDtypeStruct((2 * nchan, width), BF16),
        ),
        in_specs=specs,
        out_specs=(big, big),
        scratch_shapes=scratch,
        compiler_params=pltpu.CompilerParams(
            collective_id=0, has_side_effects=True, vmem_limit_bytes=56 * 2**20
        ),
    )(*operands)
    return jnp.dot(act, w_cat, preferred_element_type=F32).astype(BF16)


def solution(mesh):
    placed = (
        P("seq", "ch"),
        P("seq", "ch"),
        P(None, None, "seq", "ch"),
        P(),
        P(),
        P(),
        P(),
        P(),
        P(),
        P(),
        P(),
        P(),
        P(),
        P("ch"),
        P("ch", None),
    )
    return jax.shard_map(
        on_device, mesh=mesh, in_specs=placed, out_specs=P("seq", "ch"), check_vma=False
    )
```

```python
import jax
import jax.numpy as jnp
from jax import lax
from jax.experimental import pallas as pl
from jax.experimental.pallas import tpu as pltpu
from jax.sharding import PartitionSpec as P

MESH = pl.DeviceIdType.MESH
F32 = jnp.float32
BF16 = jnp.bfloat16
LANES = 128
SUB = 16
NZ = 8
NXY = 8
NX = 4
ROWS = 512
BAND = 512


def iota(shape, dim):
    return lax.broadcasted_iota(jnp.int32, shape, dim)


def one_hot(cond):
    return jnp.where(cond, 1.0, 0.0).astype(BF16)


def dot(a, b):
    return jnp.dot(a, b, preferred_element_type=F32)


def kernel(
    signal,
    gate,
    spectral,
    fwd_inner_hbm,
    fwd_middle_hbm,
    fwd_outer_hbm,
    inv_outer_hbm,
    inv_middle_hbm,
    inv_inner_hbm,
    tw_inner_hbm,
    tw_middle_hbm,
    itw_middle_hbm,
    itw_inner_hbm,
    skip,
    w_out,
    out,
    sig,
    gat,
    ker,
    silu,
    rows_a,
    send_a,
    send_z,
    recv_z,
    recv_xy,
    spec,
    send_xy2,
    recv_xy2,
    recv_z2,
    send_j,
    rows_j,
    act,
    mat_in,
    mat_inv,
    mat_m,
    mat_f,
    mat_i,
    mat_im,
    t_in,
    t_mid,
    t_imid,
    t_iin,
    factors,
    twiddles,
    wide_factor,
    column,
    act_in,
    weights,
    total,
    staged,
    small_sem,
    load_sem,
    local_sem,
    core_send,
    core_recv,
    z_send,
    z_recv,
    xy_send,
    xy_recv,
    xy2_send,
    xy2_recv,
    z2_send,
    z2_recv,
    core2_send,
    core2_recv,
    act_send,
    act_recv,
    w_send,
    w_recv,
    out_sem,
):
    nch = sig.shape[0]
    me = lax.axis_index("seq")
    ch = lax.axis_index("ch")
    core = me % 2
    chip = me // 2
    z = chip % NZ
    yx = chip // NZ
    y, x = yx // NX, yx % NX

    def at_z(d):
        other = (z + d) % NZ
        return other, ((yx * NZ + other) * 2 + core, ch)

    def at_xy(e):
        other = (y + e // NX) % 2 * NX + (x + e % NX) % NX
        return other, ((other * NZ + z) * 2 + core, ch)

    twin = (chip * 2 + 1 - core, ch)
    mate = (me, 1 - ch)

    def remote(src, dst, send, recv, device):
        return pltpu.make_async_remote_copy(
            src_ref=src,
            dst_ref=dst,
            send_sem=send,
            recv_sem=recv,
            device_id=device,
            device_id_type=MESH,
        )

    fwd_inner, fwd_middle, fwd_outer, inv_outer, inv_middle, inv_inner = range(6)
    tw_inner, tw_middle, itw_middle, itw_inner = (twiddles.at[n] for n in range(4))
    given = (
        fwd_inner_hbm,
        fwd_middle_hbm,
        fwd_outer_hbm,
        inv_outer_hbm,
        inv_middle_hbm,
        inv_inner_hbm,
    )
    given_tw = (tw_inner_hbm, tw_middle_hbm, itw_middle_hbm, itw_inner_hbm)
    factor_loads = [
        pltpu.make_async_copy(ref, factors.at[n], small_sem.at[n]) for n, ref in enumerate(given)
    ]
    tw_loads = [
        pltpu.make_async_copy(ref, twiddles.at[n], small_sem.at[6 + n])
        for n, ref in enumerate(given_tw)
    ]
    factor_loads[0].start()
    tw_loads[0].start()
    loads = []
    for i in range(nch):
        cols = pl.ds(i * LANES, LANES)
        trio = (
            pltpu.make_async_copy(signal.at[:, cols], sig.at[i], load_sem.at[0, i]),
            pltpu.make_async_copy(spectral.at[:, :, :, cols], ker.at[i], load_sem.at[1, i]),
            pltpu.make_async_copy(gate.at[:, cols], gat.at[i], load_sem.at[2, i]),
        )
        loads.append(trio)
    loads[0][0].start()
    for copy in factor_loads[1:] + tw_loads[1:]:
        copy.start()
    for i in range(1, nch):
        loads[i][0].start()

    barrier = pltpu.get_barrier_semaphore()
    pl.semaphore_signal(barrier, inc=1, device_id=twin, device_id_type=MESH)
    pl.semaphore_signal(barrier, inc=1, device_id=mate, device_id_type=MESH)
    for d in range(1, NZ):
        pl.semaphore_signal(barrier, inc=1, device_id=at_z(d)[1], device_id_type=MESH)
    for e in range(1, NXY):
        pl.semaphore_signal(barrier, inc=1, device_id=at_xy(e)[1], device_id_type=MESH)

    def digit_k(q, flip):
        half = (q >> 5) ^ flip
        return 2 * (half * SUB + (q & 15)) + ((q >> 4) & 1)

    def in_z_order(q):
        return (q & 7) * 8 + (q >> 3)

    diagonal = iota((SUB, 64 * SUB), 0) == (iota((SUB, 64 * SUB), 1) & 15)

    def expand(n, out, row_digit, col_digit):
        factor_loads[n].wait()
        place = one_hot(iota((64, 64 * SUB), 0) == col_digit(iota((64, 64 * SUB), 1) >> 4))
        wide_factor[...] = dot(factors[n], place)

        def body(t, carry):
            for u in range(8):
                q = t * 8 + u
                row = jnp.broadcast_to(wide_factor[pl.ds(row_digit(q), 1), :], (SUB, 64 * SUB))
                out[pl.ds(pl.multiple_of(q * SUB, SUB), SUB), :] = jnp.where(
                    diagonal, row, 0.0
                ).astype(BF16)
            return carry

        lax.fori_loop(0, 8, body, 0)

    def expand_four(n, out, row_digit, col_digit):
        factor_loads[n].wait()
        place = one_hot(iota((64, 256), 0) == col_digit(iota((64, 256), 1) & 63))
        pick = one_hot(iota((64, 64), 1) == row_digit(iota((64, 64), 0)))
        wide = dot(dot(pick, factors[n]).astype(BF16), place)
        for b in range(4):
            out[b * 64 : (b + 1) * 64, :] = jnp.where(
                (iota((64, 256), 1) >> 6) == b, wide, 0.0
            ).astype(BF16)

    expand_four(fwd_inner, mat_in, lambda r: digit_k(r, core), lambda s: s)
    tw_loads[0].wait()
    in_hit = iota((64, 64), 1) == digit_k(iota((64, 64), 0), core)

    def tw_in_body(t, carry):
        for u in range(8):
            n = t * 8 + u
            row = tw_inner[pl.ds(core * 32 + n, 1), :]
            col = jnp.sum(jnp.where(in_hit, row, 0.0), axis=1, keepdims=True)
            t_in[pl.ds(pl.multiple_of(n * 64, 64), 64), :] = jnp.broadcast_to(col, (64, LANES))
        return carry

    lax.fori_loop(0, 4, tw_in_body, 0)

    def stage_inner(i):
        loads[i][0].wait()

        def body(n, carry):
            base = pl.multiple_of(n * 512, 512)
            wide = jnp.concatenate(
                [sig[i, pl.ds(base, 256), :], sig[i, pl.ds(base + 256, 256), :]], axis=1
            )
            res = dot(mat_in[...], wide)
            for s in range(2):
                part = res[:, s * LANES : (s + 1) * LANES] * t_in[pl.ds(base + 256 * s, 256), :]
                part = part.astype(BF16).reshape(4, 2, 2, SUB, LANES)
                b = n * 8 + s * 4
                rows_a[i, pl.ds(core * 32 + b, 4)] = part[:, 0]
                send_a[i, pl.ds(b, 4)] = part[:, 1]
            return carry

        lax.fori_loop(0, 4, body, 0)

    def core_copy(i):
        return remote(
            send_a.at[i],
            rows_a.at[i, pl.ds(core * 32, 32)],
            core_send.at[i],
            core_recv.at[i],
            twin,
        )

    stage_inner(0)
    pl.semaphore_wait(barrier, 2 + NZ - 1 + NXY - 1)
    core_copies = [core_copy(i) for i in range(nch)]
    core_copies[0].start()
    for i in range(nch):
        loads[i][1].start()
    stage_inner(1)
    core_copies[1].start()
    expand(fwd_middle, mat_m, in_z_order, lambda s: s)
    tw_loads[1].wait()
    tm_row = tw_middle[pl.ds(chip, 1), :]
    for n in range(4):
        hit = iota((256, 64), 1) == in_z_order((iota((256, 64), 0) + n * 256) >> 4)
        col = jnp.sum(jnp.where(hit, tm_row, 0.0), axis=1, keepdims=True)
        t_mid[n * 256 : (n + 1) * 256, :] = jnp.broadcast_to(col, (256, LANES))

    def pair(ref, i):
        v = ref[i].reshape(64, 2, SUB, LANES)
        return jnp.concatenate(
            [v[:, 0].reshape(64 * SUB, LANES), v[:, 1].reshape(64 * SUB, LANES)], axis=1
        )

    def apply(matrix, wide, finish):
        def body(n, carry):
            base = pl.multiple_of(n * BAND, BAND)
            finish(n, base, dot(matrix[pl.ds(base, BAND), :], wide))
            return carry

        lax.fori_loop(0, 64 * SUB // BAND, body, 0)

    def stage_middle(i):
        core_copies[i].wait_recv()

        def finish(n, base, res):
            for p in range(2):
                part = res[:, p * LANES : (p + 1) * LANES] * t_mid[pl.ds(base, BAND), :]
                send_z[i, pl.ds(n * 4, 4), :, p] = part.astype(BF16).reshape(4, NXY, SUB, LANES)

        apply(mat_m, pair(rows_a, i), finish)

    order_z = (4, 3, 5, 2, 6, 1, 7)
    order_xy = (6, 2, 5, 7, 1, 3, 4)
    z_copies, xy_copies, xy2_copies, z2_copies = {}, {}, {}, {}

    def start_z(i):
        z_copies[i] = []
        for d in order_z:
            other, device = at_z(d)
            copy = remote(
                send_z.at[i, other], recv_z.at[i, z], z_send.at[i, d], z_recv.at[i, d], device
            )
            copy.start()
            z_copies[i].append(copy)
        own = pltpu.make_async_copy(send_z.at[i, z], recv_z.at[i, z], local_sem.at[0, i])
        own.start()
        z_copies[i].append(own)

    def start_xy(i):
        for copy in z_copies[i][:-1]:
            copy.wait_recv()
        z_copies[i][-1].wait()
        xy_copies[i] = []
        for e in order_xy:
            other, device = at_xy(e)
            copy = remote(
                recv_z.at[i, :, other],
                recv_xy.at[i, yx],
                xy_send.at[i, e],
                xy_recv.at[i, e],
                device,
            )
            copy.start()
            xy_copies[i].append(copy)
        own = pltpu.make_async_copy(recv_z.at[i, :, yx], recv_xy.at[i, yx], local_sem.at[1, i])
        own.start()
        xy_copies[i].append(own)

    def stage_outer(i):
        for copy in xy_copies[i][:-1]:
            copy.wait_recv()
        xy_copies[i][-1].wait()
        loads[i][1].wait()

        def product(n, base, res):
            factor = ker[i, pl.ds(n * 32, 32)]
            for p in range(2):
                part = res[:, p * LANES : (p + 1) * LANES].reshape(32, SUB, LANES)
                part = part * factor[:, p].astype(F32)
                spec[pl.ds(base, BAND), p * LANES : (p + 1) * LANES] = part.astype(BF16).reshape(
                    BAND, LANES
                )

        apply(mat_f, pair(recv_xy, i), product)

        def finish(n, base, res):
            for p in range(2):
                part = res[:, p * LANES : (p + 1) * LANES] * t_imid[pl.ds(base, BAND), :]
                send_xy2[i, pl.ds(n * 4, 4), :, p] = part.astype(BF16).reshape(4, NZ, SUB, LANES)

        apply(mat_i, spec[...], finish)

    def start_xy2(i):
        xy2_copies[i] = []
        for e in order_xy:
            other, device = at_xy(e)
            copy = remote(
                send_xy2.at[i, other],
                recv_xy2.at[i, yx],
                xy2_send.at[i, e],
                xy2_recv.at[i, e],
                device,
            )
            copy.start()
            xy2_copies[i].append(copy)
        own = pltpu.make_async_copy(send_xy2.at[i, yx], recv_xy2.at[i, yx], local_sem.at[2, i])
        own.start()
        xy2_copies[i].append(own)

    def start_z2(i):
        for copy in xy2_copies[i][:-1]:
            copy.wait_recv()
        xy2_copies[i][-1].wait()
        z2_copies[i] = []
        for d in order_z:
            other, device = at_z(d)
            copy = remote(
                recv_xy2.at[i, :, other],
                recv_z2.at[i, z],
                z2_send.at[i, d],
                z2_recv.at[i, d],
                device,
            )
            copy.start()
            z2_copies[i].append(copy)
        own = pltpu.make_async_copy(recv_xy2.at[i, :, z], recv_z2.at[i, z], local_sem.at[3, i])
        own.start()
        z2_copies[i].append(own)

    def core2_copy(i):
        return remote(
            send_j.at[i], rows_j.at[i, :, core], core2_send.at[i], core2_recv.at[i], twin
        )

    core2_copies = [core2_copy(i) for i in range(nch)]

    def stage_inv_middle(i):
        for copy in z2_copies[i][:-1]:
            copy.wait_recv()
        z2_copies[i][-1].wait()

        wide = pair(recv_z2, i)

        def block(n, target):
            base = pl.multiple_of(n * 256, 256)
            res = dot(mat_im[pl.ds(base, 256), :], wide)
            for p in range(2):
                part = res[:, p * LANES : (p + 1) * LANES] * t_iin[p, pl.ds(base, 256), :]
                target(n, p, part.astype(BF16).reshape(16, SUB, LANES))

        def to_twin(n, p, part):
            send_j[i, pl.ds((n - 2) * 16, 16), p] = part

        def to_own(n, p, part):
            rows_j[i, pl.ds(n * 16, 16), core, p] = part

        lax.fori_loop(2, 4, lambda n, c: (block(n, to_twin), c)[1], 0)
        core2_copies[i].start()
        lax.fori_loop(0, 2, lambda n, c: (block(n, to_own), c)[1], 0)

    def act_copy(i, n):
        at = pl.ds(pl.multiple_of(n * ROWS, ROWS), ROWS)
        return remote(
            act.at[i, at], act_in.at[i, at], act_send.at[i, n], act_recv.at[i, n], mate
        )

    def stage_inv_inner(i):
        core2_copies[i].wait_recv()
        scale = skip[pl.ds(i * LANES, LANES)].reshape(1, LANES)

        def body(n, carry):
            base = pl.multiple_of(n * 512, 512)
            left = rows_j[i, pl.ds(n * 8, 4)].reshape(256, LANES)
            right = rows_j[i, pl.ds(n * 8 + 4, 4)].reshape(256, LANES)
            res = dot(mat_inv[...], jnp.concatenate([left, right], axis=1))
            for s in range(2):
                at = pl.ds(base + 256 * s, 256)
                conv = res[:, s * LANES : (s + 1) * LANES]
                conv = conv + scale * sig[i, at, :].astype(F32)
                act[i, at, :] = (silu[i, at, :] * conv).astype(BF16)
            act_copy(i, n).start()
            return carry

        lax.fori_loop(0, 4, body, 0)

    def out_copy(n):
        at = pl.ds(pl.multiple_of(n * ROWS, ROWS), ROWS)
        return pltpu.make_async_copy(staged.at[at], out.at[at], out_sem.at[n])

    def project(step, parts):
        def body(n, carry):
            at = pl.ds(pl.multiple_of(n * ROWS, ROWS), ROWS)
            for ref, i in parts:
                if ref is act_in:
                    act_copy(i, n).wait_recv()
            wide = jnp.concatenate([ref[i, at, :] for ref, i in parts], axis=1)
            for c in range(0, width, 256):
                res = dot(wide, weights[step * 256 : (step + 1) * 256, c : c + 256])
                if step > 0:
                    res = res + total[at, c : c + 256]
                if step < 2:
                    total[at, c : c + 256] = res
                else:
                    staged[at, c : c + 256] = res.astype(BF16)
            if step == 2:
                out_copy(n).start()
            return carry

        lax.fori_loop(0, sig.shape[1] // ROWS, body, 0)

    def make_silu(i):
        loads[i][2].wait()

        def body(n, carry):
            at = pl.ds(pl.multiple_of(n * 256, 256), 256)
            g = gat[i, at, :].astype(F32)
            silu[i, at, :] = g / (1.0 + jnp.exp(-g))
            return carry

        lax.fori_loop(0, 8, body, 0)

    def tw_imid():
        tw_loads[2].wait()
        hit = iota((64, 64), 1) == chip
        col = jnp.sum(jnp.where(hit, itw_middle[...], 0.0), axis=1, keepdims=True)
        column[...] = jnp.broadcast_to(col, (64, LANES))

        def body(t, carry):
            for u in range(8):
                n = t * 8 + u
                t_imid[pl.ds(pl.multiple_of(n * SUB, SUB), SUB), :] = jnp.broadcast_to(
                    column[pl.ds(n, 1), :], (SUB, LANES)
                )
            return carry

        lax.fori_loop(0, 8, body, 0)

    def tw_iin():
        tw_loads[3].wait()
        hits = [
            iota((SUB, 64), 1) == 2 * (core * SUB + iota((SUB, 64), 0)) + p for p in range(2)
        ]

        def body(t, carry):
            for u in range(8):
                n = t * 8 + u
                row = itw_inner[pl.ds((t // 4 + core) % 2 * 32 + n % 32, 1), :]
                for p in range(2):
                    col = jnp.sum(jnp.where(hits[p], row, 0.0), axis=1, keepdims=True)
                    t_iin[p, pl.ds(pl.multiple_of(n * SUB, SUB), SUB), :] = jnp.broadcast_to(
                        col, (SUB, LANES)
                    )
            return carry

        lax.fori_loop(0, 8, body, 0)

    stage_middle(0)
    start_z(0)
    stage_inner(2)
    core_copies[2].start()
    depth, width = weights.shape[0] // 2, weights.shape[1]
    w_copy = remote(
        w_out.at[:, pl.ds(pl.multiple_of((1 - ch) * width, width), width)],
        weights.at[pl.ds(depth, depth)],
        w_send,
        w_recv,
        mate,
    )
    w_copy.start()
    w_own = pltpu.make_async_copy(
        w_out.at[:, pl.ds(pl.multiple_of(ch * width, width), width)],
        weights.at[pl.ds(0, depth)],
        small_sem.at[10],
    )
    w_own.start()
    for i in range(nch):
        loads[i][2].start()
    stage_middle(1)
    stage_middle(2)
    expand(fwd_outer, mat_f, lambda q: q, lambda s: s)
    expand(inv_outer, mat_i, lambda q: q, lambda s: s)
    tw_imid()
    start_z(1)
    start_xy(0)
    expand(inv_middle, mat_im, lambda q: (q // 32 + core) % 2 * 32 + q % 32, in_z_order)
    expand_four(inv_inner, mat_inv, lambda r: r, lambda s: digit_k(s, 0))
    tw_iin()
    for i in range(nch):
        make_silu(i)
    stage_outer(0)
    start_xy2(0)
    start_z(2)
    start_xy(1)
    stage_outer(1)
    start_xy2(1)
    start_z2(0)
    start_xy(2)
    start_z2(1)
    stage_outer(2)
    start_xy2(2)
    stage_inv_middle(0)
    stage_inv_inner(0)
    start_z2(2)
    w_own.wait()
    stage_inv_middle(1)
    stage_inv_inner(1)
    project(0, ((act, 0), (act, 1)))
    stage_inv_middle(2)
    stage_inv_inner(2)
    w_copy.wait_recv()
    project(1, ((act, 2), (act_in, 0)))
    project(2, ((act_in, 1), (act_in, 2)))

    for i in range(nch):
        core_copies[i].wait_send()
        core2_copies[i].wait_send()
        for table in (z_copies, xy_copies, xy2_copies, z2_copies):
            for copy in table[i][:-1]:
                copy.wait_send()
        for n in range(sig.shape[1] // ROWS):
            act_copy(i, n).wait_send()
    w_copy.wait_send()
    for n in range(sig.shape[1] // ROWS):
        out_copy(n).wait()


def on_device(*args):
    signal, w_out = args[0], args[14]
    tokens, nchan = signal.shape
    nch = nchan // LANES
    width = w_out.shape[1] // 2
    big = pl.BlockSpec(memory_space=pl.ANY)
    specs = [big] * 13 + [pl.BlockSpec(memory_space=pltpu.VMEM), big]
    chunk = (nch, 64, 2, SUB, LANES)
    square = pltpu.VMEM((64 * SUB, 64 * SUB), BF16)
    dma = pltpu.SemaphoreType.DMA
    scratch = [
        pltpu.VMEM((nch, tokens, LANES), BF16),
        pltpu.VMEM((nch, tokens, LANES), BF16),
        pltpu.VMEM(chunk, BF16),
        pltpu.VMEM((nch, tokens, LANES), F32),
        pltpu.VMEM(chunk, BF16),
        pltpu.VMEM((nch, 32, 2, SUB, LANES), BF16),
        pltpu.VMEM((nch, NZ, NXY, 2, SUB, LANES), BF16),
        pltpu.VMEM((nch, NZ, NXY, 2, SUB, LANES), BF16),
        pltpu.VMEM((nch, NXY, NZ, 2, SUB, LANES), BF16),
        pltpu.VMEM((64 * SUB, 2 * LANES), BF16),
        pltpu.VMEM((nch, NXY, NZ, 2, SUB, LANES), BF16),
        pltpu.VMEM((nch, NXY, NZ, 2, SUB, LANES), BF16),
        pltpu.VMEM((nch, NZ, NXY, 2, SUB, LANES), BF16),
        pltpu.VMEM((nch, 32, 2, SUB, LANES), BF16),
        pltpu.VMEM((nch, 32, 2, 2, SUB, LANES), BF16),
        pltpu.VMEM((nch, tokens, LANES), BF16),
        pltpu.VMEM((256, 256), BF16),
        pltpu.VMEM((256, 256), BF16),
        square,
        square,
        square,
        square,
        pltpu.VMEM((tokens, LANES), F32),
        pltpu.VMEM((64 * SUB, LANES), F32),
        pltpu.VMEM((64 * SUB, LANES), F32),
        pltpu.VMEM((2, 64 * SUB, LANES), F32),
        pltpu.VMEM((6, 64, 64), BF16),
        pltpu.VMEM((4, 64, 64), F32),
        pltpu.VMEM((64, 64 * SUB), F32),
        pltpu.VMEM((64, LANES), F32),
        pltpu.VMEM((nch, tokens, LANES), BF16),
        pltpu.VMEM((2 * nchan, width), BF16),
        pltpu.VMEM((tokens, width), F32),
        pltpu.VMEM((tokens, width), BF16),
        dma((11,)),
        dma((3, nch)),
        dma((4, nch)),
        dma((nch,)),
        dma((nch,)),
        dma((nch, NZ)),
        dma((nch, NZ)),
        dma((nch, NXY)),
        dma((nch, NXY)),
        dma((nch, NXY)),
        dma((nch, NXY)),
        dma((nch, NZ)),
        dma((nch, NZ)),
        dma((nch,)),
        dma((nch,)),
        dma((nch, tokens // ROWS)),
        dma((nch, tokens // ROWS)),
        dma(()),
        dma(()),
        dma((tokens // ROWS,)),
    ]
    return pl.pallas_call(
        kernel,
        out_shape=jax.ShapeDtypeStruct((tokens, width), BF16),
        in_specs=specs,
        out_specs=big,
        scratch_shapes=scratch,
        compiler_params=pltpu.CompilerParams(
            collective_id=0, has_side_effects=True, vmem_limit_bytes=56 * 2**20
        ),
    )(*args)


def solution(mesh):
    placed = (
        P("seq", "ch"),
        P("seq", "ch"),
        P(None, None, "seq", "ch"),
        P(),
        P(),
        P(),
        P(),
        P(),
        P(),
        P(),
        P(),
        P(),
        P(),
        P("ch"),
        P("ch", None),
    )
    return jax.shard_map(
        on_device, mesh=mesh, in_specs=placed, out_specs=P("seq", "ch"), check_vma=False
    )
```

```python
import jax
import jax.numpy as jnp
from jax import lax
from jax.experimental import pallas as pl
from jax.experimental.pallas import tpu as pltpu
from jax.sharding import PartitionSpec as P

MESH = pl.DeviceIdType.MESH
F32 = jnp.float32
BF16 = jnp.bfloat16
LANES = 128
SUB = 16
NZ = 8
NXY = 8
NX = 4
ROWS = 512
HAND = 256
BAND = 512


def iota(shape, dim):
    return lax.broadcasted_iota(jnp.int32, shape, dim)


def one_hot(cond):
    return jnp.where(cond, 1.0, 0.0).astype(BF16)


def dot(a, b):
    return jnp.dot(a, b, preferred_element_type=F32)


def kernel(
    signal,
    gate,
    spectral,
    fwd_inner_hbm,
    fwd_middle_hbm,
    fwd_outer_hbm,
    inv_outer_hbm,
    inv_middle_hbm,
    inv_inner_hbm,
    tw_inner_hbm,
    tw_middle_hbm,
    itw_middle_hbm,
    itw_inner_hbm,
    skip,
    w_out,
    out,
    sig,
    gat,
    ker,
    silu,
    rows_a,
    send_a,
    send_z,
    recv_z,
    recv_xy,
    spec,
    send_xy2,
    recv_xy2,
    recv_z2,
    send_j,
    rows_j,
    act,
    mat_in,
    mat_inv,
    mat_m,
    mat_f,
    mat_i,
    mat_im,
    t_in,
    t_mid,
    t_imid,
    t_iin,
    factors,
    twiddles,
    wide_factor,
    column,
    act_in,
    weights,
    total,
    staged,
    small_sem,
    signal_sem,
    load_sem,
    core_send,
    core_recv,
    z_send,
    z_recv,
    xy_send,
    xy_recv,
    xy2_send,
    xy2_recv,
    z2_send,
    z2_recv,
    core2_send,
    core2_recv,
    act_send,
    act_recv,
    w_send,
    w_recv,
    out_sem,
):
    nch = sig.shape[0]
    me = lax.axis_index("seq")
    ch = lax.axis_index("ch")
    core = me % 2
    chip = me // 2
    z = chip % NZ
    yx = chip // NZ
    y, x = yx // NX, yx % NX

    def at_z(d):
        other = (z + d) % NZ
        return other, ((yx * NZ + other) * 2 + core, ch)

    def at_xy(e):
        other = (y + e // NX) % 2 * NX + (x + e % NX) % NX
        return other, ((other * NZ + z) * 2 + core, ch)

    twin = (chip * 2 + 1 - core, ch)
    mate = (me, 1 - ch)

    def remote(src, dst, send, recv, device):
        return pltpu.make_async_remote_copy(
            src_ref=src,
            dst_ref=dst,
            send_sem=send,
            recv_sem=recv,
            device_id=device,
            device_id_type=MESH,
        )

    fwd_inner, fwd_middle, fwd_outer, inv_outer, inv_middle, inv_inner = range(6)
    tw_inner, tw_middle, itw_middle, itw_inner = (twiddles.at[n] for n in range(4))
    given = (
        fwd_inner_hbm,
        fwd_middle_hbm,
        fwd_outer_hbm,
        inv_outer_hbm,
        inv_middle_hbm,
        inv_inner_hbm,
    )
    given_tw = (tw_inner_hbm, tw_middle_hbm, itw_middle_hbm, itw_inner_hbm)
    factor_loads = [
        pltpu.make_async_copy(ref, factors.at[n], small_sem.at[n]) for n, ref in enumerate(given)
    ]
    tw_loads = [
        pltpu.make_async_copy(ref, twiddles.at[n], small_sem.at[6 + n])
        for n, ref in enumerate(given_tw)
    ]
    def signal_load(i, n):
        at = pl.ds(pl.multiple_of(n * ROWS, ROWS), ROWS)
        return pltpu.make_async_copy(
            signal.at[at, pl.ds(i * LANES, LANES)], sig.at[i, at], signal_sem.at[i, n]
        )

    for n in range(4):
        signal_load(0, n).start()
    factor_loads[0].start()
    tw_loads[0].start()
    loads = []
    for i in range(nch):
        cols = pl.ds(i * LANES, LANES)
        pair_of_loads = (
            pltpu.make_async_copy(spectral.at[:, :, :, cols], ker.at[i], load_sem.at[0, i]),
            pltpu.make_async_copy(gate.at[:, cols], gat.at[i], load_sem.at[1, i]),
        )
        loads.append(pair_of_loads)
    for copy in factor_loads[1:] + tw_loads[1:]:
        copy.start()
    for i in range(1, nch):
        for n in range(4):
            signal_load(i, n).start()

    barrier = pltpu.get_barrier_semaphore()
    pl.semaphore_signal(barrier, inc=1, device_id=twin, device_id_type=MESH)
    pl.semaphore_signal(barrier, inc=1, device_id=mate, device_id_type=MESH)
    for d in range(1, NZ):
        pl.semaphore_signal(barrier, inc=1, device_id=at_z(d)[1], device_id_type=MESH)
    for e in range(1, NXY):
        pl.semaphore_signal(barrier, inc=1, device_id=at_xy(e)[1], device_id_type=MESH)

    def digit_k(q, flip):
        half = (q >> 5) ^ flip
        return 2 * (half * SUB + (q & 15)) + ((q >> 4) & 1)

    def in_z_order(q):
        return (q & 7) * 8 + (q >> 3)

    diagonal = iota((SUB, 64 * SUB), 0) == (iota((SUB, 64 * SUB), 1) & 15)

    def expand(n, out, row_digit, col_digit):
        factor_loads[n].wait()
        place = one_hot(iota((64, 64 * SUB), 0) == col_digit(iota((64, 64 * SUB), 1) >> 4))
        wide_factor[...] = dot(factors[n], place)

        def body(t, carry):
            for u in range(8):
                q = t * 8 + u
                row = jnp.broadcast_to(wide_factor[pl.ds(row_digit(q), 1), :], (SUB, 64 * SUB))
                out[pl.ds(pl.multiple_of(q * SUB, SUB), SUB), :] = jnp.where(
                    diagonal, row, 0.0
                ).astype(BF16)
            return carry

        lax.fori_loop(0, 8, body, 0)

    def expand_four(n, out, row_digit, col_digit):
        factor_loads[n].wait()
        place = one_hot(iota((64, 256), 0) == col_digit(iota((64, 256), 1) & 63))
        pick = one_hot(iota((64, 64), 1) == row_digit(iota((64, 64), 0)))
        wide = dot(dot(pick, factors[n]).astype(BF16), place)
        for b in range(4):
            out[b * 64 : (b + 1) * 64, :] = jnp.where(
                (iota((64, 256), 1) >> 6) == b, wide, 0.0
            ).astype(BF16)

    expand_four(fwd_inner, mat_in, lambda r: digit_k(r, core), lambda s: s)
    tw_loads[0].wait()
    in_hit = iota((64, 64), 1) == digit_k(iota((64, 64), 0), core)

    def tw_in_body(t, carry):
        for u in range(8):
            n = t * 8 + u
            row = tw_inner[pl.ds(core * 32 + n, 1), :]
            col = jnp.sum(jnp.where(in_hit, row, 0.0), axis=1, keepdims=True)
            t_in[pl.ds(pl.multiple_of(n * 64, 64), 64), :] = jnp.broadcast_to(col, (64, LANES))
        return carry

    lax.fori_loop(0, 4, tw_in_body, 0)

    def stage_inner(i):
        def body(n, carry):
            signal_load(i, n).wait()
            base = pl.multiple_of(n * 512, 512)
            wide = jnp.concatenate(
                [sig[i, pl.ds(base, 256), :], sig[i, pl.ds(base + 256, 256), :]], axis=1
            )
            res = dot(mat_in[...], wide)
            for s in range(2):
                part = res[:, s * LANES : (s + 1) * LANES] * t_in[pl.ds(base + 256 * s, 256), :]
                part = part.astype(BF16).reshape(4, 2, 2, SUB, LANES)
                b = n * 8 + s * 4
                rows_a[i, pl.ds(core * 32 + b, 4)] = part[:, 0]
                send_a[i, pl.ds(b, 4)] = part[:, 1]
            return carry

        lax.fori_loop(0, 4, body, 0)

    def core_copy(i):
        return remote(
            send_a.at[i],
            rows_a.at[i, pl.ds(core * 32, 32)],
            core_send.at[i],
            core_recv.at[i],
            twin,
        )

    stage_inner(0)
    pl.semaphore_wait(barrier, 2 + NZ - 1 + NXY - 1)
    core_copies = [core_copy(i) for i in range(nch)]
    core_copies[0].start()
    for i in range(nch):
        loads[i][0].start()
    stage_inner(1)
    core_copies[1].start()
    expand(fwd_middle, mat_m, in_z_order, lambda s: s)
    tw_loads[1].wait()
    tm_row = tw_middle[pl.ds(chip, 1), :]
    for n in range(4):
        hit = iota((256, 64), 1) == in_z_order((iota((256, 64), 0) + n * 256) >> 4)
        col = jnp.sum(jnp.where(hit, tm_row, 0.0), axis=1, keepdims=True)
        t_mid[n * 256 : (n + 1) * 256, :] = jnp.broadcast_to(col, (256, LANES))

    def pair(ref, i):
        v = ref[i].reshape(64, 2, SUB, LANES)
        return jnp.concatenate(
            [v[:, 0].reshape(64 * SUB, LANES), v[:, 1].reshape(64 * SUB, LANES)], axis=1
        )

    def apply(matrix, wide, finish):
        def body(n, carry):
            base = pl.multiple_of(n * BAND, BAND)
            finish(n, base, dot(matrix[pl.ds(base, BAND), :], wide))
            return carry

        lax.fori_loop(0, 64 * SUB // BAND, body, 0)

    def stage_middle(i):
        core_copies[i].wait_recv()

        def finish(n, base, res):
            for p in range(2):
                part = res[:, p * LANES : (p + 1) * LANES] * t_mid[pl.ds(base, BAND), :]
                send_z[i, pl.ds(n * 4, 4), :, p] = part.astype(BF16).reshape(4, NXY, SUB, LANES)

        apply(mat_m, pair(rows_a, i), finish)

    order_z = (4, 3, 5, 2, 6, 1, 7)
    order_xy = (6, 2, 5, 7, 1, 3, 4)
    z_copies, xy_copies, xy2_copies, z2_copies = {}, {}, {}, {}

    def start_z(i):
        z_copies[i] = []
        for d in order_z:
            other, device = at_z(d)
            copy = remote(
                send_z.at[i, other], recv_z.at[i, z], z_send.at[i, d], z_recv.at[i, d], device
            )
            copy.start()
            z_copies[i].append(copy)
        recv_z[i, z] = send_z[i, z]

    def start_xy(i):
        for copy in z_copies[i]:
            copy.wait_recv()
        xy_copies[i] = []
        for e in order_xy:
            other, device = at_xy(e)
            copy = remote(
                recv_z.at[i, :, other],
                recv_xy.at[i, yx],
                xy_send.at[i, e],
                xy_recv.at[i, e],
                device,
            )
            copy.start()
            xy_copies[i].append(copy)
        recv_xy[i, yx] = recv_z[i, :, yx]

    def stage_outer(i):
        for copy in xy_copies[i]:
            copy.wait_recv()
        loads[i][0].wait()

        def product(n, base, res):
            factor = ker[i, pl.ds(n * 32, 32)]
            for p in range(2):
                part = res[:, p * LANES : (p + 1) * LANES].reshape(32, SUB, LANES)
                part = part * factor[:, p].astype(F32)
                spec[pl.ds(base, BAND), p * LANES : (p + 1) * LANES] = part.astype(BF16).reshape(
                    BAND, LANES
                )

        apply(mat_f, pair(recv_xy, i), product)

        def finish(n, base, res):
            for p in range(2):
                part = res[:, p * LANES : (p + 1) * LANES] * t_imid[pl.ds(base, BAND), :]
                send_xy2[i, pl.ds(n * 4, 4), :, p] = part.astype(BF16).reshape(4, NZ, SUB, LANES)

        apply(mat_i, spec[...], finish)

    def start_xy2(i):
        xy2_copies[i] = []
        for e in order_xy:
            other, device = at_xy(e)
            copy = remote(
                send_xy2.at[i, other],
                recv_xy2.at[i, yx],
                xy2_send.at[i, e],
                xy2_recv.at[i, e],
                device,
            )
            copy.start()
            xy2_copies[i].append(copy)
        recv_xy2[i, yx] = send_xy2[i, yx]

    def start_z2(i):
        for copy in xy2_copies[i]:
            copy.wait_recv()
        z2_copies[i] = []
        for d in order_z:
            other, device = at_z(d)
            copy = remote(
                recv_xy2.at[i, :, other],
                recv_z2.at[i, z],
                z2_send.at[i, d],
                z2_recv.at[i, d],
                device,
            )
            copy.start()
            z2_copies[i].append(copy)
        recv_z2[i, z] = recv_xy2[i, :, z]

    def core2_copy(i):
        return remote(
            send_j.at[i], rows_j.at[i, :, core], core2_send.at[i], core2_recv.at[i], twin
        )

    core2_copies = [core2_copy(i) for i in range(nch)]

    def stage_inv_middle(i):
        for copy in z2_copies[i]:
            copy.wait_recv()

        wide = pair(recv_z2, i)

        def block(n, target):
            base = pl.multiple_of(n * 256, 256)
            res = dot(mat_im[pl.ds(base, 256), :], wide)
            for p in range(2):
                part = res[:, p * LANES : (p + 1) * LANES] * t_iin[p, pl.ds(base, 256), :]
                target(n, p, part.astype(BF16).reshape(16, SUB, LANES))

        def to_twin(n, p, part):
            send_j[i, pl.ds((n - 2) * 16, 16), p] = part

        def to_own(n, p, part):
            rows_j[i, pl.ds(n * 16, 16), core, p] = part

        lax.fori_loop(2, 4, lambda n, c: (block(n, to_twin), c)[1], 0)
        core2_copies[i].start()
        lax.fori_loop(0, 2, lambda n, c: (block(n, to_own), c)[1], 0)

    def act_copy(i, n):
        at = pl.ds(pl.multiple_of(n * ROWS, ROWS), ROWS)
        return remote(
            act.at[i, at], act_in.at[i, at], act_send.at[i, n], act_recv.at[i, n], mate
        )

    def stage_inv_inner(i):
        core2_copies[i].wait_recv()
        scale = skip[pl.ds(i * LANES, LANES)].reshape(1, LANES)

        def body(n, carry):
            base = pl.multiple_of(n * 512, 512)
            left = rows_j[i, pl.ds(n * 8, 4)].reshape(256, LANES)
            right = rows_j[i, pl.ds(n * 8 + 4, 4)].reshape(256, LANES)
            res = dot(mat_inv[...], jnp.concatenate([left, right], axis=1))
            for s in range(2):
                at = pl.ds(base + 256 * s, 256)
                conv = res[:, s * LANES : (s + 1) * LANES]
                conv = conv + scale * sig[i, at, :].astype(F32)
                act[i, at, :] = (silu[i, at, :] * conv).astype(BF16)
            act_copy(i, n).start()
            return carry

        lax.fori_loop(0, 4, body, 0)

    def out_copy(n):
        at = pl.ds(pl.multiple_of(n * ROWS, ROWS), ROWS)
        return pltpu.make_async_copy(staged.at[at], out.at[at], out_sem.at[n])

    def project(step, parts):
        def body(n, carry):
            at = pl.ds(pl.multiple_of(n * ROWS, ROWS), ROWS)
            for ref, i in parts:
                if ref is act_in:
                    act_copy(i, n).wait_recv()
            wide = jnp.concatenate([ref[i, at, :] for ref, i in parts], axis=1)
            for c in range(0, width, 256):
                res = dot(wide, weights[step * 256 : (step + 1) * 256, c : c + 256])
                if step > 0:
                    res = res + total[at, c : c + 256]
                if step < 2:
                    total[at, c : c + 256] = res
                else:
                    staged[at, c : c + 256] = res.astype(BF16)
            if step == 2:
                out_copy(n).start()
            return carry

        lax.fori_loop(0, sig.shape[1] // ROWS, body, 0)

    def make_silu(i):
        loads[i][1].wait()

        def body(n, carry):
            at = pl.ds(pl.multiple_of(n * 256, 256), 256)
            g = gat[i, at, :].astype(F32)
            silu[i, at, :] = g / (1.0 + jnp.exp(-g))
            return carry

        lax.fori_loop(0, 8, body, 0)

    def tw_imid():
        tw_loads[2].wait()
        hit = iota((64, 64), 1) == chip
        col = jnp.sum(jnp.where(hit, itw_middle[...], 0.0), axis=1, keepdims=True)
        column[...] = jnp.broadcast_to(col, (64, LANES))

        def body(t, carry):
            for u in range(8):
                n = t * 8 + u
                t_imid[pl.ds(pl.multiple_of(n * SUB, SUB), SUB), :] = jnp.broadcast_to(
                    column[pl.ds(n, 1), :], (SUB, LANES)
                )
            return carry

        lax.fori_loop(0, 8, body, 0)

    def tw_iin():
        tw_loads[3].wait()
        hits = [
            iota((SUB, 64), 1) == 2 * (core * SUB + iota((SUB, 64), 0)) + p for p in range(2)
        ]

        def body(t, carry):
            for u in range(8):
                n = t * 8 + u
                row = itw_inner[pl.ds((t // 4 + core) % 2 * 32 + n % 32, 1), :]
                for p in range(2):
                    col = jnp.sum(jnp.where(hits[p], row, 0.0), axis=1, keepdims=True)
                    t_iin[p, pl.ds(pl.multiple_of(n * SUB, SUB), SUB), :] = jnp.broadcast_to(
                        col, (SUB, LANES)
                    )
            return carry

        lax.fori_loop(0, 8, body, 0)

    stage_middle(0)
    start_z(0)
    stage_inner(2)
    core_copies[2].start()
    depth, width = weights.shape[0] // 2, weights.shape[1]
    w_copy = remote(
        w_out.at[:, pl.ds(pl.multiple_of((1 - ch) * width, width), width)],
        weights.at[pl.ds(depth, depth)],
        w_send,
        w_recv,
        mate,
    )
    w_copy.start()
    w_own = pltpu.make_async_copy(
        w_out.at[:, pl.ds(pl.multiple_of(ch * width, width), width)],
        weights.at[pl.ds(0, depth)],
        small_sem.at[10],
    )
    w_own.start()
    for i in range(nch):
        loads[i][1].start()
    stage_middle(1)
    stage_middle(2)
    expand(fwd_outer, mat_f, lambda q: q, lambda s: s)
    expand(inv_outer, mat_i, lambda q: q, lambda s: s)
    tw_imid()
    start_z(1)
    start_xy(0)
    expand(inv_middle, mat_im, lambda q: (q // 32 + core) % 2 * 32 + q % 32, in_z_order)
    expand_four(inv_inner, mat_inv, lambda r: r, lambda s: digit_k(s, 0))
    tw_iin()
    for i in range(nch):
        make_silu(i)
    stage_outer(0)
    start_xy2(0)
    start_z(2)
    start_xy(1)
    stage_outer(1)
    start_xy2(1)
    start_z2(0)
    start_xy(2)
    start_z2(1)
    stage_outer(2)
    start_xy2(2)
    stage_inv_middle(0)
    stage_inv_inner(0)
    start_z2(2)
    w_own.wait()
    stage_inv_middle(1)
    stage_inv_inner(1)
    stage_inv_middle(2)
    stage_inv_inner(2)
    project(0, ((act, 0), (act, 1)))
    w_copy.wait_recv()
    project(1, ((act, 2), (act_in, 0)))
    project(2, ((act_in, 1), (act_in, 2)))

    for i in range(nch):
        core_copies[i].wait_send()
        core2_copies[i].wait_send()
        for table in (z_copies, xy_copies, xy2_copies, z2_copies):
            for copy in table[i]:
                copy.wait_send()
        for n in range(sig.shape[1] // ROWS):
            act_copy(i, n).wait_send()
    w_copy.wait_send()
    for n in range(sig.shape[1] // ROWS):
        out_copy(n).wait()


def hand_on(source, out, held, read_sem, write_sem):
    blocks = [pl.ds(n * HAND, HAND) for n in range(source.shape[0] // HAND)]
    reads = [
        pltpu.make_async_copy(source.at[at], held.at[at], read_sem.at[n])
        for n, at in enumerate(blocks)
    ]
    writes = [
        pltpu.make_async_copy(held.at[at], out.at[at], write_sem.at[n])
        for n, at in enumerate(blocks)
    ]
    for copy in reads:
        copy.start()
    for read, write in zip(reads, writes):
        read.wait()
        write.start()
    for copy in writes:
        copy.wait()


def on_device(*args):
    signal, w_out = args[0], args[14]
    tokens, nchan = signal.shape
    nch = nchan // LANES
    width = w_out.shape[1] // 2
    big = pl.BlockSpec(memory_space=pl.ANY)
    specs = [big] * 13 + [pl.BlockSpec(memory_space=pltpu.VMEM), big]
    chunk = (nch, 64, 2, SUB, LANES)
    square = pltpu.VMEM((64 * SUB, 64 * SUB), BF16)
    dma = pltpu.SemaphoreType.DMA
    scratch = [
        pltpu.VMEM((nch, tokens, LANES), BF16),
        pltpu.VMEM((nch, tokens, LANES), BF16),
        pltpu.VMEM(chunk, BF16),
        pltpu.VMEM((nch, tokens, LANES), F32),
        pltpu.VMEM(chunk, BF16),
        pltpu.VMEM((nch, 32, 2, SUB, LANES), BF16),
        pltpu.VMEM((nch, NZ, NXY, 2, SUB, LANES), BF16),
        pltpu.VMEM((nch, NZ, NXY, 2, SUB, LANES), BF16),
        pltpu.VMEM((nch, NXY, NZ, 2, SUB, LANES), BF16),
        pltpu.VMEM((64 * SUB, 2 * LANES), BF16),
        pltpu.VMEM((nch, NXY, NZ, 2, SUB, LANES), BF16),
        pltpu.VMEM((nch, NXY, NZ, 2, SUB, LANES), BF16),
        pltpu.VMEM((nch, NZ, NXY, 2, SUB, LANES), BF16),
        pltpu.VMEM((nch, 32, 2, SUB, LANES), BF16),
        pltpu.VMEM((nch, 32, 2, 2, SUB, LANES), BF16),
        pltpu.VMEM((nch, tokens, LANES), BF16),
        pltpu.VMEM((256, 256), BF16),
        pltpu.VMEM((256, 256), BF16),
        square,
        square,
        square,
        square,
        pltpu.VMEM((tokens, LANES), F32),
        pltpu.VMEM((64 * SUB, LANES), F32),
        pltpu.VMEM((64 * SUB, LANES), F32),
        pltpu.VMEM((2, 64 * SUB, LANES), F32),
        pltpu.VMEM((6, 64, 64), BF16),
        pltpu.VMEM((4, 64, 64), F32),
        pltpu.VMEM((64, 64 * SUB), F32),
        pltpu.VMEM((64, LANES), F32),
        pltpu.VMEM((nch, tokens, LANES), BF16),
        pltpu.VMEM((2 * nchan, width), BF16),
        pltpu.VMEM((tokens, width), F32),
        pltpu.VMEM((tokens, width), BF16),
        dma((11,)),
        dma((nch, tokens // ROWS)),
        dma((2, nch)),
        dma((nch,)),
        dma((nch,)),
        dma((nch, NZ)),
        dma((nch, NZ)),
        dma((nch, NXY)),
        dma((nch, NXY)),
        dma((nch, NXY)),
        dma((nch, NXY)),
        dma((nch, NZ)),
        dma((nch, NZ)),
        dma((nch,)),
        dma((nch,)),
        dma((nch, tokens // ROWS)),
        dma((nch, tokens // ROWS)),
        dma(()),
        dma(()),
        dma((tokens // ROWS,)),
    ]
    mixed = pl.pallas_call(
        kernel,
        out_shape=jax.ShapeDtypeStruct((tokens, width), BF16),
        in_specs=specs,
        out_specs=big,
        scratch_shapes=scratch,
        compiler_params=pltpu.CompilerParams(
            collective_id=0, has_side_effects=True, vmem_limit_bytes=56 * 2**20
        ),
    )(*args)
    return pl.pallas_call(
        hand_on,
        out_shape=jax.ShapeDtypeStruct((tokens, width), BF16),
        in_specs=[big],
        out_specs=big,
        scratch_shapes=[
            pltpu.VMEM((tokens, width), BF16),
            dma((tokens // HAND,)),
            dma((tokens // HAND,)),
        ],
        compiler_params=pltpu.CompilerParams(vmem_limit_bytes=60 * 2**20),
    )(mixed)


def solution(mesh):
    placed = (
        P("seq", "ch"),
        P("seq", "ch"),
        P(None, None, "seq", "ch"),
        P(),
        P(),
        P(),
        P(),
        P(),
        P(),
        P(),
        P(),
        P(),
        P(),
        P("ch"),
        P("ch", None),
    )
    return jax.shard_map(
        on_device, mesh=mesh, in_specs=placed, out_specs=P("seq", "ch"), check_vma=False
    )
```

```python
import jax
import jax.numpy as jnp
from jax import lax
from jax.experimental import pallas as pl
from jax.experimental.pallas import tpu as pltpu
from jax.sharding import PartitionSpec as P

MESH = pl.DeviceIdType.MESH
F32 = jnp.float32
BF16 = jnp.bfloat16
LANES = 128
SUB = 16
NZ = 8
NXY = 8
NX = 4
ROWS = 512
HAND = 256
BAND = 512


def iota(shape, dim):
    return lax.broadcasted_iota(jnp.int32, shape, dim)


def one_hot(cond):
    return jnp.where(cond, 1.0, 0.0).astype(BF16)


def dot(a, b):
    return jnp.dot(a, b, preferred_element_type=F32)


def kernel(
    signal,
    gate,
    spectral,
    fwd_inner_hbm,
    fwd_middle_hbm,
    fwd_outer_hbm,
    inv_outer_hbm,
    inv_middle_hbm,
    inv_inner_hbm,
    tw_inner_hbm,
    tw_middle_hbm,
    itw_middle_hbm,
    itw_inner_hbm,
    skip,
    w_out,
    out,
    sig,
    gat,
    ker,
    silu,
    rows_a,
    send_a,
    send_z,
    recv_z,
    recv_xy,
    spec,
    send_xy2,
    recv_xy2,
    recv_z2,
    send_j,
    rows_j,
    act,
    mat_in,
    mat_inv,
    mat_m,
    mat_f,
    mat_i,
    mat_im,
    t_in,
    t_mid,
    t_imid,
    t_iin,
    factors,
    twiddles,
    wide_factor,
    column,
    act_in,
    weights,
    total,
    staged,
    small_sem,
    signal_sem,
    load_sem,
    core_send,
    core_recv,
    z_send,
    z_recv,
    xy_send,
    xy_recv,
    xy2_send,
    xy2_recv,
    z2_send,
    z2_recv,
    core2_send,
    core2_recv,
    act_send,
    act_recv,
    w_send,
    w_recv,
    out_sem,
):
    nch = sig.shape[0]
    me = lax.axis_index("seq")
    ch = lax.axis_index("ch")
    core = me % 2
    chip = me // 2
    z = chip % NZ
    yx = chip // NZ
    y, x = yx // NX, yx % NX

    def at_z(d):
        other = (z + d) % NZ
        return other, ((yx * NZ + other) * 2 + core, ch)

    def at_xy(e):
        other = (y + e // NX) % 2 * NX + (x + e % NX) % NX
        return other, ((other * NZ + z) * 2 + core, ch)

    twin = (chip * 2 + 1 - core, ch)
    mate = (me, 1 - ch)

    def remote(src, dst, send, recv, device):
        return pltpu.make_async_remote_copy(
            src_ref=src,
            dst_ref=dst,
            send_sem=send,
            recv_sem=recv,
            device_id=device,
            device_id_type=MESH,
        )

    fwd_inner, fwd_middle, fwd_outer, inv_outer, inv_middle, inv_inner = range(6)
    tw_inner, tw_middle, itw_middle, itw_inner = (twiddles.at[n] for n in range(4))
    given = (
        fwd_inner_hbm,
        fwd_middle_hbm,
        fwd_outer_hbm,
        inv_outer_hbm,
        inv_middle_hbm,
        inv_inner_hbm,
    )
    given_tw = (tw_inner_hbm, tw_middle_hbm, itw_middle_hbm, itw_inner_hbm)
    factor_loads = [
        pltpu.make_async_copy(ref, factors.at[n], small_sem.at[n]) for n, ref in enumerate(given)
    ]
    tw_loads = [
        pltpu.make_async_copy(ref, twiddles.at[n], small_sem.at[6 + n])
        for n, ref in enumerate(given_tw)
    ]
    def signal_load(i, n):
        at = pl.ds(pl.multiple_of(n * ROWS, ROWS), ROWS)
        return pltpu.make_async_copy(
            signal.at[at, pl.ds(i * LANES, LANES)], sig.at[i, at], signal_sem.at[i, n]
        )

    for n in range(4):
        signal_load(0, n).start()
    factor_loads[0].start()
    tw_loads[0].start()
    loads = []
    for i in range(nch):
        cols = pl.ds(i * LANES, LANES)
        pair_of_loads = (
            pltpu.make_async_copy(spectral.at[:, :, :, cols], ker.at[i], load_sem.at[0, i]),
            pltpu.make_async_copy(gate.at[:, cols], gat.at[i], load_sem.at[1, i]),
        )
        loads.append(pair_of_loads)
    for copy in factor_loads[1:] + tw_loads[1:]:
        copy.start()
    for i in range(1, nch):
        for n in range(4):
            signal_load(i, n).start()

    barrier = pltpu.get_barrier_semaphore()
    pl.semaphore_signal(barrier, inc=1, device_id=twin, device_id_type=MESH)
    pl.semaphore_signal(barrier, inc=1, device_id=mate, device_id_type=MESH)
    for d in range(1, NZ):
        pl.semaphore_signal(barrier, inc=1, device_id=at_z(d)[1], device_id_type=MESH)
    for e in range(1, NXY):
        pl.semaphore_signal(barrier, inc=1, device_id=at_xy(e)[1], device_id_type=MESH)

    def digit_k(q, flip):
        half = (q >> 5) ^ flip
        return 2 * (half * SUB + (q & 15)) + ((q >> 4) & 1)

    def in_z_order(q):
        return (q & 7) * 8 + (q >> 3)

    diagonal = iota((SUB, 64 * SUB), 0) == (iota((SUB, 64 * SUB), 1) & 15)

    def expand(n, out, row_digit, col_digit):
        factor_loads[n].wait()
        place = one_hot(iota((64, 64 * SUB), 0) == col_digit(iota((64, 64 * SUB), 1) >> 4))
        wide_factor[...] = dot(factors[n], place)

        def body(t, carry):
            for u in range(8):
                q = t * 8 + u
                row = jnp.broadcast_to(wide_factor[pl.ds(row_digit(q), 1), :], (SUB, 64 * SUB))
                out[pl.ds(pl.multiple_of(q * SUB, SUB), SUB), :] = jnp.where(
                    diagonal, row, 0.0
                ).astype(BF16)
            return carry

        lax.fori_loop(0, 8, body, 0)

    def expand_four(n, out, row_digit, col_digit):
        factor_loads[n].wait()
        place = one_hot(iota((64, 256), 0) == col_digit(iota((64, 256), 1) & 63))
        pick = one_hot(iota((64, 64), 1) == row_digit(iota((64, 64), 0)))
        wide = dot(dot(pick, factors[n]).astype(BF16), place)
        for b in range(4):
            out[b * 64 : (b + 1) * 64, :] = jnp.where(
                (iota((64, 256), 1) >> 6) == b, wide, 0.0
            ).astype(BF16)

    expand_four(fwd_inner, mat_in, lambda r: digit_k(r, core), lambda s: s)
    tw_loads[0].wait()
    in_hit = iota((64, 64), 1) == digit_k(iota((64, 64), 0), core)

    def tw_in_body(t, carry):
        for u in range(8):
            n = t * 8 + u
            row = tw_inner[pl.ds(core * 32 + n, 1), :]
            col = jnp.sum(jnp.where(in_hit, row, 0.0), axis=1, keepdims=True)
            t_in[pl.ds(pl.multiple_of(n * 64, 64), 64), :] = jnp.broadcast_to(col, (64, LANES))
        return carry

    lax.fori_loop(0, 4, tw_in_body, 0)

    def stage_inner(i):
        def body(n, carry):
            signal_load(i, n).wait()
            base = pl.multiple_of(n * 512, 512)
            wide = jnp.concatenate(
                [sig[i, pl.ds(base, 256), :], sig[i, pl.ds(base + 256, 256), :]], axis=1
            )
            res = dot(mat_in[...], wide)
            for s in range(2):
                part = res[:, s * LANES : (s + 1) * LANES] * t_in[pl.ds(base + 256 * s, 256), :]
                part = part.astype(BF16).reshape(4, 2, 2, SUB, LANES)
                b = n * 8 + s * 4
                rows_a[i, pl.ds(core * 32 + b, 4)] = part[:, 0]
                send_a[i, pl.ds(b, 4)] = part[:, 1]
            return carry

        lax.fori_loop(0, 4, body, 0)

    def core_copy(i):
        return remote(
            send_a.at[i],
            rows_a.at[i, pl.ds(core * 32, 32)],
            core_send.at[i],
            core_recv.at[i],
            twin,
        )

    stage_inner(0)
    pl.semaphore_wait(barrier, 2 + NZ - 1 + NXY - 1)
    core_copies = [core_copy(i) for i in range(nch)]
    core_copies[0].start()
    for i in range(nch):
        loads[i][0].start()
    stage_inner(1)
    core_copies[1].start()
    expand(fwd_middle, mat_m, in_z_order, lambda s: s)
    tw_loads[1].wait()
    tm_row = tw_middle[pl.ds(chip, 1), :]
    for n in range(4):
        hit = iota((256, 64), 1) == in_z_order((iota((256, 64), 0) + n * 256) >> 4)
        col = jnp.sum(jnp.where(hit, tm_row, 0.0), axis=1, keepdims=True)
        t_mid[n * 256 : (n + 1) * 256, :] = jnp.broadcast_to(col, (256, LANES))

    def pair(ref, i):
        v = ref[i].reshape(64, 2, SUB, LANES)
        return jnp.concatenate(
            [v[:, 0].reshape(64 * SUB, LANES), v[:, 1].reshape(64 * SUB, LANES)], axis=1
        )

    def apply(matrix, wide, finish):
        def body(n, carry):
            base = pl.multiple_of(n * BAND, BAND)
            finish(n, base, dot(matrix[pl.ds(base, BAND), :], wide))
            return carry

        lax.fori_loop(0, 64 * SUB // BAND, body, 0)

    def stage_middle(i):
        core_copies[i].wait_recv()

        def finish(n, base, res):
            for p in range(2):
                part = res[:, p * LANES : (p + 1) * LANES] * t_mid[pl.ds(base, BAND), :]
                send_z[i, pl.ds(n * 4, 4), :, p] = part.astype(BF16).reshape(4, NXY, SUB, LANES)

        apply(mat_m, pair(rows_a, i), finish)

    order_z = (4, 3, 5, 2, 6, 1, 7)
    order_xy = (6, 2, 5, 7, 1, 3, 4)
    z_copies, xy_copies, xy2_copies, z2_copies = {}, {}, {}, {}

    def start_z(i):
        z_copies[i] = []
        for d in order_z:
            other, device = at_z(d)
            copy = remote(
                send_z.at[i, other], recv_z.at[i, z], z_send.at[i, d], z_recv.at[i, d], device
            )
            copy.start()
            z_copies[i].append(copy)
        recv_z[i, z] = send_z[i, z]

    def start_xy(i):
        for copy in z_copies[i]:
            copy.wait_recv()
        xy_copies[i] = []
        for e in order_xy:
            other, device = at_xy(e)
            copy = remote(
                recv_z.at[i, :, other],
                recv_xy.at[i, yx],
                xy_send.at[i, e],
                xy_recv.at[i, e],
                device,
            )
            copy.start()
            xy_copies[i].append(copy)
        recv_xy[i, yx] = recv_z[i, :, yx]

    def stage_outer(i):
        for copy in xy_copies[i]:
            copy.wait_recv()
        loads[i][0].wait()

        def product(n, base, res):
            factor = ker[i, pl.ds(n * 32, 32)]
            for p in range(2):
                part = res[:, p * LANES : (p + 1) * LANES].reshape(32, SUB, LANES)
                part = part * factor[:, p].astype(F32)
                spec[pl.ds(base, BAND), p * LANES : (p + 1) * LANES] = part.astype(BF16).reshape(
                    BAND, LANES
                )

        apply(mat_f, pair(recv_xy, i), product)

        def finish(n, base, res):
            for p in range(2):
                part = res[:, p * LANES : (p + 1) * LANES] * t_imid[pl.ds(base, BAND), :]
                send_xy2[i, pl.ds(n * 4, 4), :, p] = part.astype(BF16).reshape(4, NZ, SUB, LANES)

        apply(mat_i, spec[...], finish)

    def start_xy2(i):
        xy2_copies[i] = []
        for e in order_xy:
            other, device = at_xy(e)
            copy = remote(
                send_xy2.at[i, other],
                recv_xy2.at[i, yx],
                xy2_send.at[i, e],
                xy2_recv.at[i, e],
                device,
            )
            copy.start()
            xy2_copies[i].append(copy)
        recv_xy2[i, yx] = send_xy2[i, yx]

    def start_z2(i):
        for copy in xy2_copies[i]:
            copy.wait_recv()
        z2_copies[i] = []
        for d in order_z:
            other, device = at_z(d)
            copy = remote(
                recv_xy2.at[i, :, other],
                recv_z2.at[i, z],
                z2_send.at[i, d],
                z2_recv.at[i, d],
                device,
            )
            copy.start()
            z2_copies[i].append(copy)
        recv_z2[i, z] = recv_xy2[i, :, z]

    def core2_copy(i, h):
        at = pl.ds(h * 16, 16)
        return remote(
            send_j.at[i, at],
            rows_j.at[i, at, core],
            core2_send.at[i, h],
            core2_recv.at[i, h],
            twin,
        )

    def stage_inv_middle(i):
        for copy in z2_copies[i]:
            copy.wait_recv()

        wide = pair(recv_z2, i)

        def block(n, target):
            base = pl.multiple_of(n * 256, 256)
            res = dot(mat_im[pl.ds(base, 256), :], wide)
            for p in range(2):
                part = res[:, p * LANES : (p + 1) * LANES] * t_iin[p, pl.ds(base, 256), :]
                target(n, p, part.astype(BF16).reshape(16, SUB, LANES))

        def to_twin(n, p, part):
            send_j[i, pl.ds((n - 2) * 16, 16), p] = part

        def to_own(n, p, part):
            rows_j[i, pl.ds(n * 16, 16), core, p] = part

        for h in range(2):
            block(2 + h, to_twin)
            core2_copy(i, h).start()
        lax.fori_loop(0, 2, lambda n, c: (block(n, to_own), c)[1], 0)

    def act_copy(i, n):
        at = pl.ds(pl.multiple_of(n * ROWS, ROWS), ROWS)
        return remote(
            act.at[i, at], act_in.at[i, at], act_send.at[i, n], act_recv.at[i, n], mate
        )

    def stage_inv_inner(i):
        scale = skip[pl.ds(i * LANES, LANES)].reshape(1, LANES)

        def body(n, carry):
            base = pl.multiple_of(n * 512, 512)
            left = rows_j[i, pl.ds(n * 8, 4)].reshape(256, LANES)
            right = rows_j[i, pl.ds(n * 8 + 4, 4)].reshape(256, LANES)
            res = dot(mat_inv[...], jnp.concatenate([left, right], axis=1))
            for s in range(2):
                at = pl.ds(base + 256 * s, 256)
                conv = res[:, s * LANES : (s + 1) * LANES]
                conv = conv + scale * sig[i, at, :].astype(F32)
                act[i, at, :] = (silu[i, at, :] * conv).astype(BF16)
            act_copy(i, n).start()
            return carry

        for h in range(2):
            core2_copy(i, h).wait_recv()
            lax.fori_loop(2 * h, 2 * h + 2, body, 0)

    def out_copy(n):
        at = pl.ds(pl.multiple_of(n * ROWS, ROWS), ROWS)
        return pltpu.make_async_copy(staged.at[at], out.at[at], out_sem.at[n])

    def project(step, parts):
        def body(n, carry):
            at = pl.ds(pl.multiple_of(n * ROWS, ROWS), ROWS)
            for ref, i in parts:
                if ref is act_in:
                    act_copy(i, n).wait_recv()
            wide = jnp.concatenate([ref[i, at, :] for ref, i in parts], axis=1)
            for c in range(0, width, 256):
                res = dot(wide, weights[step * 256 : (step + 1) * 256, c : c + 256])
                if step > 0:
                    res = res + total[at, c : c + 256]
                if step < 2:
                    total[at, c : c + 256] = res
                else:
                    staged[at, c : c + 256] = res.astype(BF16)
            if step == 2:
                out_copy(n).start()
            return carry

        lax.fori_loop(0, sig.shape[1] // ROWS, body, 0)

    def make_silu(i):
        loads[i][1].wait()

        def body(n, carry):
            at = pl.ds(pl.multiple_of(n * 256, 256), 256)
            g = gat[i, at, :].astype(F32)
            silu[i, at, :] = g / (1.0 + jnp.exp(-g))
            return carry

        lax.fori_loop(0, 8, body, 0)

    def tw_imid():
        tw_loads[2].wait()
        hit = iota((64, 64), 1) == chip
        col = jnp.sum(jnp.where(hit, itw_middle[...], 0.0), axis=1, keepdims=True)
        column[...] = jnp.broadcast_to(col, (64, LANES))

        def body(t, carry):
            for u in range(8):
                n = t * 8 + u
                t_imid[pl.ds(pl.multiple_of(n * SUB, SUB), SUB), :] = jnp.broadcast_to(
                    column[pl.ds(n, 1), :], (SUB, LANES)
                )
            return carry

        lax.fori_loop(0, 8, body, 0)

    def tw_iin():
        tw_loads[3].wait()
        hits = [
            iota((SUB, 64), 1) == 2 * (core * SUB + iota((SUB, 64), 0)) + p for p in range(2)
        ]

        def body(t, carry):
            for u in range(8):
                n = t * 8 + u
                row = itw_inner[pl.ds((t // 4 + core) % 2 * 32 + n % 32, 1), :]
                for p in range(2):
                    col = jnp.sum(jnp.where(hits[p], row, 0.0), axis=1, keepdims=True)
                    t_iin[p, pl.ds(pl.multiple_of(n * SUB, SUB), SUB), :] = jnp.broadcast_to(
                        col, (SUB, LANES)
                    )
            return carry

        lax.fori_loop(0, 8, body, 0)

    stage_middle(0)
    start_z(0)
    stage_inner(2)
    core_copies[2].start()
    depth, width = weights.shape[0] // 2, weights.shape[1]
    w_copy = remote(
        w_out.at[:, pl.ds(pl.multiple_of((1 - ch) * width, width), width)],
        weights.at[pl.ds(depth, depth)],
        w_send,
        w_recv,
        mate,
    )
    w_copy.start()
    w_own = pltpu.make_async_copy(
        w_out.at[:, pl.ds(pl.multiple_of(ch * width, width), width)],
        weights.at[pl.ds(0, depth)],
        small_sem.at[10],
    )
    w_own.start()
    for i in range(nch):
        loads[i][1].start()
    stage_middle(1)
    stage_middle(2)
    expand(fwd_outer, mat_f, lambda q: q, lambda s: s)
    expand(inv_outer, mat_i, lambda q: q, lambda s: s)
    tw_imid()
    start_z(1)
    start_xy(0)
    expand(inv_middle, mat_im, lambda q: (q // 32 + core) % 2 * 32 + q % 32, in_z_order)
    expand_four(inv_inner, mat_inv, lambda r: r, lambda s: digit_k(s, 0))
    tw_iin()
    for i in range(nch):
        make_silu(i)
    stage_outer(0)
    start_xy2(0)
    start_z(2)
    start_xy(1)
    stage_outer(1)
    start_xy2(1)
    start_z2(0)
    start_xy(2)
    start_z2(1)
    stage_outer(2)
    start_xy2(2)
    stage_inv_middle(0)
    stage_inv_inner(0)
    start_z2(2)
    w_own.wait()
    stage_inv_middle(1)
    stage_inv_inner(1)
    stage_inv_middle(2)
    stage_inv_inner(2)
    project(0, ((act, 0), (act, 1)))
    w_copy.wait_recv()
    project(1, ((act, 2), (act_in, 0)))
    project(2, ((act_in, 1), (act_in, 2)))

    for i in range(nch):
        core_copies[i].wait_send()
        for h in range(2):
            core2_copy(i, h).wait_send()
        for table in (z_copies, xy_copies, xy2_copies, z2_copies):
            for copy in table[i]:
                copy.wait_send()
        for n in range(sig.shape[1] // ROWS):
            act_copy(i, n).wait_send()
    w_copy.wait_send()
    for n in range(sig.shape[1] // ROWS):
        out_copy(n).wait()


def hand_on(source, out, held, read_sem, write_sem):
    blocks = [pl.ds(n * HAND, HAND) for n in range(source.shape[0] // HAND)]
    reads = [
        pltpu.make_async_copy(source.at[at], held.at[at], read_sem.at[n])
        for n, at in enumerate(blocks)
    ]
    writes = [
        pltpu.make_async_copy(held.at[at], out.at[at], write_sem.at[n])
        for n, at in enumerate(blocks)
    ]
    for copy in reads:
        copy.start()
    for read, write in zip(reads, writes):
        read.wait()
        write.start()
    for copy in writes:
        copy.wait()


def on_device(*args):
    signal, w_out = args[0], args[14]
    tokens, nchan = signal.shape
    nch = nchan // LANES
    width = w_out.shape[1] // 2
    big = pl.BlockSpec(memory_space=pl.ANY)
    specs = [big] * 13 + [pl.BlockSpec(memory_space=pltpu.VMEM), big]
    chunk = (nch, 64, 2, SUB, LANES)
    square = pltpu.VMEM((64 * SUB, 64 * SUB), BF16)
    dma = pltpu.SemaphoreType.DMA
    scratch = [
        pltpu.VMEM((nch, tokens, LANES), BF16),
        pltpu.VMEM((nch, tokens, LANES), BF16),
        pltpu.VMEM(chunk, BF16),
        pltpu.VMEM((nch, tokens, LANES), F32),
        pltpu.VMEM(chunk, BF16),
        pltpu.VMEM((nch, 32, 2, SUB, LANES), BF16),
        pltpu.VMEM((nch, NZ, NXY, 2, SUB, LANES), BF16),
        pltpu.VMEM((nch, NZ, NXY, 2, SUB, LANES), BF16),
        pltpu.VMEM((nch, NXY, NZ, 2, SUB, LANES), BF16),
        pltpu.VMEM((64 * SUB, 2 * LANES), BF16),
        pltpu.VMEM((nch, NXY, NZ, 2, SUB, LANES), BF16),
        pltpu.VMEM((nch, NXY, NZ, 2, SUB, LANES), BF16),
        pltpu.VMEM((nch, NZ, NXY, 2, SUB, LANES), BF16),
        pltpu.VMEM((nch, 32, 2, SUB, LANES), BF16),
        pltpu.VMEM((nch, 32, 2, 2, SUB, LANES), BF16),
        pltpu.VMEM((nch, tokens, LANES), BF16),
        pltpu.VMEM((256, 256), BF16),
        pltpu.VMEM((256, 256), BF16),
        square,
        square,
        square,
        square,
        pltpu.VMEM((tokens, LANES), F32),
        pltpu.VMEM((64 * SUB, LANES), F32),
        pltpu.VMEM((64 * SUB, LANES), F32),
        pltpu.VMEM((2, 64 * SUB, LANES), F32),
        pltpu.VMEM((6, 64, 64), BF16),
        pltpu.VMEM((4, 64, 64), F32),
        pltpu.VMEM((64, 64 * SUB), F32),
        pltpu.VMEM((64, LANES), F32),
        pltpu.VMEM((nch, tokens, LANES), BF16),
        pltpu.VMEM((2 * nchan, width), BF16),
        pltpu.VMEM((tokens, width), F32),
        pltpu.VMEM((tokens, width), BF16),
        dma((11,)),
        dma((nch, tokens // ROWS)),
        dma((2, nch)),
        dma((nch,)),
        dma((nch,)),
        dma((nch, NZ)),
        dma((nch, NZ)),
        dma((nch, NXY)),
        dma((nch, NXY)),
        dma((nch, NXY)),
        dma((nch, NXY)),
        dma((nch, NZ)),
        dma((nch, NZ)),
        dma((nch, 2)),
        dma((nch, 2)),
        dma((nch, tokens // ROWS)),
        dma((nch, tokens // ROWS)),
        dma(()),
        dma(()),
        dma((tokens // ROWS,)),
    ]
    mixed = pl.pallas_call(
        kernel,
        out_shape=jax.ShapeDtypeStruct((tokens, width), BF16),
        in_specs=specs,
        out_specs=big,
        scratch_shapes=scratch,
        compiler_params=pltpu.CompilerParams(
            collective_id=0, has_side_effects=True, vmem_limit_bytes=56 * 2**20
        ),
    )(*args)
    return pl.pallas_call(
        hand_on,
        out_shape=jax.ShapeDtypeStruct((tokens, width), BF16),
        in_specs=[big],
        out_specs=big,
        scratch_shapes=[
            pltpu.VMEM((tokens, width), BF16),
            dma((tokens // HAND,)),
            dma((tokens // HAND,)),
        ],
        compiler_params=pltpu.CompilerParams(vmem_limit_bytes=60 * 2**20),
    )(mixed)


def solution(mesh):
    placed = (
        P("seq", "ch"),
        P("seq", "ch"),
        P(None, None, "seq", "ch"),
        P(),
        P(),
        P(),
        P(),
        P(),
        P(),
        P(),
        P(),
        P(),
        P(),
        P("ch"),
        P("ch", None),
    )
    return jax.shard_map(
        on_device, mesh=mesh, in_specs=placed, out_specs=P("seq", "ch"), check_vma=False
    )
```
